32 devices in a mesh: section: 16 (over z, x, core), tensor: 2 (over y).
Axes of the slice: x: 2, y: 2, z: 4, core: 2. Of those that a mesh axis runs over, the one named last changes fastest.
Arguments:
- forward_input: bfloat16 [16, 256, 8192], P('section', None, 'tensor'), may hold values from -6 to 6
- saved_last: bfloat16 [16, 256, 8192], P('section', None, 'tensor'), may hold values from -6 to 6
- saved_first: bfloat16 [16, 256, 8192], P('section', None, 'tensor'), may hold values from -6 to 6
- first_cotangent: bfloat16 [16, 256, 8192], P('section', None, 'tensor'), may hold values from -6 to 6
- section_entry: bfloat16 [256, 8192], P(None, 'tensor'), may hold values from -6 to 6
- last_gain: float32 [16, 8192], P('section'), may hold values from 0.1 to 1.9
- last_up: bfloat16 [16, 8192, 1024], P('section', None, 'tensor'), may hold values from -0.0625 to 0.0625
- last_down: bfloat16 [16, 1024, 8192], P('section', 'tensor'), may hold values from -0.1875 to 0.1875
- first_gain: float32 [16, 8192], P('section'), may hold values from 0.1 to 1.9
- first_up: bfloat16 [16, 8192, 1024], P('section', None, 'tensor'), may hold values from -0.0625 to 0.0625
- first_down: bfloat16 [16, 1024, 8192], P('section', 'tensor'), may hold values from -0.1875 to 0.1875
- head_gain: float32 [8192], replicated, may hold values from 0.1 to 1.9
- head_weight: float32 [8192, 4], P('tensor'), may hold values from -0.0625 to 0.0625
- head_bias: float32 [4], replicated, may hold values from -3 to 3
- prompt_length: int32 [1], replicated, may hold values from 8 to 248
- keep_mask: int32 [1, 256], replicated, may hold values 0 or 1
- target_box: int32 [1, 4], replicated, may hold values from 0 to 1000, as said below
Outputs:
- layer_output: bfloat16 [16, 256, 8192], P('section', None, 'tensor')
- input_gradient: bfloat16 [16, 256, 8192], P('section', None, 'tensor')
The draws below stay inside these ranges and needn't reach their ends.
Inputs may be any that keep to these rules, and one draw needn't show every extreme that they name: `target_box`: each row is a box x1, y1, x2, y2 with x2 - x1 and y2 - y1 at least 100.
All inputs are finite; a program needn't handle non-finite values.
Results may differ from the reference program's by a relative error of at most 0.018.
Values may be sent and summed in bfloat16 or wider, within the bound.
No kernel may reach another device: no remote copies, remote signals or barrier semaphores. Data moves between devices by JAX's collectives and lax.ppermute only.
A program may use at most 128 MiB of HBM per device.

```python
import jax
import jax.numpy as jnp
from jax import lax

D = 8192
HID = 1024
SEQ = 256
MB_ROWS = 1
TOKENS = 256
N_SECTION = 16
N_TENSOR = 2


def draw_target_box(key, part):
    key_list = jax.random.split(key, 4)
    corner_x = jnp.maximum(jax.random.randint(key_list[0], (MB_ROWS,), 0, 1000) - 100, 0)
    corner_y = jnp.maximum(jax.random.randint(key_list[1], (MB_ROWS,), 0, 1000) - 100, 0)
    extent_x = jax.random.randint(key_list[2], (MB_ROWS,), 100, 1001)
    extent_y = jax.random.randint(key_list[3], (MB_ROWS,), 100, 1001)
    far_x = jnp.minimum(corner_x + extent_x, 1000)
    far_y = jnp.minimum(corner_y + extent_y, 1000)
    return jnp.stack([corner_x, corner_y, far_x, far_y], axis=1).astype(jnp.int32)


def plant(result, stream_key, smallest, high):
    place = [jax.random.randint(jax.random.fold_in(stream_key, axis), (), 0, length) for axis, length in enumerate(result.shape)]
    longest = result.shape.index(max(result.shape))
    next_to = place[:longest] + [(place[longest] + 1) % result.shape[longest]] + place[longest + 1:]
    return result.at[tuple(place)].set(smallest).at[tuple(next_to)].set(high)


def steps_of(rng, shape, pieces, smallest, top_value):
    loudness, own = 1.0, jax.random.fold_in(rng, 6)
    for axis_at, blocks in pieces:
        heights = jnp.exp(jax.random.uniform(jax.random.fold_in(own, axis_at), (blocks,), jnp.float32, smallest / len(pieces), top_value / len(pieces)))
        loudness = loudness * jnp.repeat(heights, shape[axis_at] // blocks).reshape([-1 if axis == axis_at else 1 for axis in range(len(shape))])
    return loudness


def scatter_about(key, shape, scale, reach, cuts=(), kind=jnp.bfloat16):
    entries = scale * jax.random.normal(key, shape, jnp.float32)
    if cuts:
        entries = entries * steps_of(key, shape, cuts, -0.22, 0.18)
    return jnp.clip(entries, -reach, reach).astype(kind)


def setup_inputs(seed: int = 0) -> dict:
    key_of = jax.random.split(jax.random.key(seed), 18)
    forward_input = scatter_about(key_of[0], (N_SECTION, TOKENS, D), 1.0, 6.0, ((0, 16), (2, 2)))
    saved_last = scatter_about(key_of[1], (N_SECTION, TOKENS, D), 1.0, 6.0, ((0, 16), (2, 2)))
    saved_first = scatter_about(key_of[2], (N_SECTION, TOKENS, D), 1.0, 6.0, ((0, 16), (2, 2)))
    first_cotangent = scatter_about(key_of[3], (N_SECTION, TOKENS, D), 1.0, 6.0, ((0, 16), (2, 2)))
    section_entry = scatter_about(key_of[4], (TOKENS, D), 1.0, 6.0, ((1, 2),))
    last_gain = jnp.clip(1.0 + 0.18 * jax.random.normal(key_of[5], (N_SECTION, D), jnp.float32), 0.1, 1.9)
    last_up = scatter_about(key_of[6], (N_SECTION, D, HID), D ** -0.5, 0.0625, ((0, 16), (2, 2)))
    last_down = scatter_about(key_of[7], (N_SECTION, HID, D), HID ** -0.5, 0.1875, ((0, 16), (1, 2)))
    first_gain = jnp.clip(1.0 + 0.18 * jax.random.normal(key_of[8], (N_SECTION, D), jnp.float32), 0.1, 1.9)
    first_up = scatter_about(key_of[9], (N_SECTION, D, HID), D ** -0.5, 0.0625, ((0, 16), (2, 2)))
    first_down = scatter_about(key_of[10], (N_SECTION, HID, D), HID ** -0.5, 0.1875, ((0, 16), (1, 2)))
    head_gain = jnp.clip(1.0 + 0.18 * jax.random.normal(key_of[11], (D,), jnp.float32), 0.1, 1.9)
    head_weight = scatter_about(key_of[12], (D, 4), D ** -0.5, 0.0625, ((0, 2),), jnp.float32)
    head_bias = scatter_about(key_of[13], (4,), 1.0, 3.0, (), jnp.float32)
    prompt_length = jax.random.randint(key_of[14], (MB_ROWS,), 8, SEQ - 7).astype(jnp.int32)
    keep_mask = plant((jax.random.randint(key_of[15], (MB_ROWS, SEQ), 0, 4) < 1).astype(jnp.int32), jax.random.fold_in(key_of[15], 1), 0, 1)
    target_box = draw_target_box(jax.random.fold_in(key_of[17], 71), 0)
    return {"forward_input": forward_input, "saved_last": saved_last, "saved_first": saved_first, "first_cotangent": first_cotangent, "section_entry": section_entry, "last_gain": last_gain, "last_up": last_up, "last_down": last_down, "first_gain": first_gain, "first_up": first_up, "first_down": first_down, "head_gain": head_gain, "head_weight": head_weight, "head_bias": head_bias, "prompt_length": prompt_length, "keep_mask": keep_mask, "target_box": target_box}


epsilon = 1e-06
softness = 4.0
loss_scale = 4096.0

def unit_rows(values):
    values = values.astype(jnp.float32)
    inverse = lax.rsqrt(lax.optimization_barrier(jnp.mean(values * values, axis=-1, keepdims=True)) + epsilon)
    return (values * inverse, inverse)

def grouped_product(left, right, transpose_right):
    group_width = left.shape[1] // N_TENSOR
    out_width = right.shape[0] if transpose_right else right.shape[1]
    total_sum = jnp.zeros((left.shape[0], out_width), jnp.float32)
    for group in range(N_TENSOR):
        piece_left = left[:, group * group_width:(group + 1) * group_width]
        if transpose_right:
            piece_right = right[:, group * group_width:(group + 1) * group_width].T
        else:
            piece_right = right[group * group_width:(group + 1) * group_width, :]
        term = jnp.dot(piece_left, piece_right, preferred_element_type=jnp.float32).astype(jnp.bfloat16)
        total_sum = total_sum + lax.optimization_barrier(term).astype(jnp.float32)
    return total_sum

def layer_apply(values, gain_row, up_matrix, down_matrix):
    scaled, inverse = unit_rows(values)
    normed = (scaled * gain_row).astype(jnp.bfloat16)
    activated = jax.nn.silu(jnp.dot(normed, up_matrix, preferred_element_type=jnp.float32)).astype(jnp.bfloat16)
    return (values.astype(jnp.float32) + grouped_product(activated, down_matrix, False)).astype(jnp.bfloat16)

def layer_grad(values, cotangent, gain_row, up_matrix, down_matrix):
    scaled, inverse = unit_rows(values)
    normed = (scaled * gain_row).astype(jnp.bfloat16)
    pre_act = jnp.dot(normed, up_matrix, preferred_element_type=jnp.float32)
    act_grad = jnp.dot(cotangent, down_matrix.T, preferred_element_type=jnp.float32)
    sigmoid_pre = jax.nn.sigmoid(pre_act)
    pre_grad = (act_grad * sigmoid_pre * (1.0 + pre_act * (1.0 - sigmoid_pre))).astype(jnp.bfloat16)
    norm_grad = grouped_product(pre_grad, up_matrix, True)
    projection = lax.optimization_barrier(jnp.mean(scaled * gain_row * norm_grad, axis=-1, keepdims=True))
    return (cotangent.astype(jnp.float32) + inverse * (gain_row * norm_grad - scaled * projection)).astype(jnp.bfloat16)

def soft_min(first, second):
    return 0.5 * (first + second - jnp.sqrt((first - second) * (first - second) + softness * softness))

def soft_max(first, second):
    return 0.5 * (first + second + jnp.sqrt((first - second) * (first - second) + softness * softness))

def soft_relu(difference):
    return 0.5 * (difference + jnp.sqrt(difference * difference + softness * softness))

def box_loss(logits, target_box):
    scaled_box = jax.nn.sigmoid(logits) * 1000.0
    centre_x = scaled_box[:, 0]
    centre_y = scaled_box[:, 1]
    box_width = scaled_box[:, 2]
    box_height = scaled_box[:, 3]
    left_pred = centre_x - 0.5 * box_width
    right_pred = centre_x + 0.5 * box_width
    lower_pred = centre_y - 0.5 * box_height
    upper_pred = centre_y + 0.5 * box_height
    target = target_box.astype(jnp.float32)
    inner_width = soft_relu(soft_min(right_pred, target[:, 2]) - soft_max(left_pred, target[:, 0]))
    inner_height = soft_relu(soft_min(upper_pred, target[:, 3]) - soft_max(lower_pred, target[:, 1]))
    intersection_area = inner_width * inner_height
    target_area = (target[:, 2] - target[:, 0]) * (target[:, 3] - target[:, 1])
    union_area = box_width * box_height + target_area - intersection_area
    outer_width = soft_max(right_pred, target[:, 2]) - soft_min(left_pred, target[:, 0])
    outer_height = soft_max(upper_pred, target[:, 3]) - soft_min(lower_pred, target[:, 1])
    enclosing = outer_width * outer_height
    return loss_scale * jnp.mean(1.0 - intersection_area / union_area + (enclosing - union_area) / enclosing)

def pool_table(prompt_length, keep_mask):
    positions = jnp.arange(keep_mask.shape[1], dtype=jnp.int32)[None, :]
    starts = prompt_length[:, None]
    weights = (positions == starts - 1).astype(jnp.float32) + (positions >= starts).astype(jnp.float32) * keep_mask.astype(jnp.float32)
    return (weights, lax.optimization_barrier(jnp.sum(weights, axis=1)))

def head_value(final_hidden, head_gain, head_weight, head_bias, weights, counts, target_box):
    tokens = final_hidden.reshape(weights.shape[0], weights.shape[1], final_hidden.shape[1])
    pooled = jnp.einsum('rt,rtd->rd', weights, tokens, precision=lax.Precision.HIGHEST) / counts[:, None]
    scaled, inverse = unit_rows(pooled)
    logits = jnp.dot(scaled * head_gain, head_weight, precision=lax.Precision.HIGHEST) + head_bias
    return box_loss(logits, target_box)

def reference(forward_input, saved_last, saved_first, first_cotangent, section_entry, last_gain, last_up, last_down, first_gain, first_up, first_down, head_gain, head_weight, head_bias, prompt_length, keep_mask, target_box):
    section_count = forward_input.shape[0]
    hidden = [layer_apply(forward_input[section], last_gain[section], last_up[section], last_down[section]) for section in range(section_count)]
    outputs = []
    for section in range(section_count):
        entry = section_entry if section == 0 else hidden[section - 1]
        outputs.append(layer_apply(entry, first_gain[section], first_up[section], first_down[section]))
    weights, counts = pool_table(prompt_length, keep_mask)
    closing = section_count - 1

    def loss_of(final_hidden):
        return head_value(final_hidden, head_gain, head_weight, head_bias, weights, counts, target_box)
    loss_value, pullback = jax.vjp(loss_of, hidden[closing].astype(jnp.float32))
    head_cotangent = pullback(jnp.ones((), jnp.float32))[0].astype(jnp.bfloat16)
    gradients = []
    for section in range(section_count):
        if section == closing:
            saved = forward_input[section]
            cotangent = head_cotangent
        else:
            saved = saved_last[section]
            cotangent = layer_grad(saved_first[section + 1], first_cotangent[section + 1], first_gain[section + 1], first_up[section + 1], first_down[section + 1])
        gradients.append(layer_grad(saved, cotangent, last_gain[section], last_up[section], last_down[section]))
    return (jnp.stack(outputs), jnp.stack(gradients))
```

```python
import jax
import jax.numpy as jnp
from jax import lax
from jax.sharding import PartitionSpec as P

epsilon = 1e-06
softness = 4.0
loss_scale = 4096.0
chunk_width = 1024

f32 = jnp.float32
bf16 = jnp.bfloat16


def shifted(value, axis, steps):
    count = lax.axis_size(axis)
    initial, last = (max(0, -steps), min(count, count - steps))
    return lax.ppermute(value, axis, [(source, source + steps) for source in range(initial, last)])


def rotated(value, steps):
    count = lax.axis_size("tensor")
    return lax.ppermute(value, "tensor", [(i, (i + steps) % count) for i in range(count)])


class Lane:
    def __init__(self, depth):
        self.depth = depth
        self.past = []

    def send(self, value, steps):
        if len(self.past) >= self.depth:
            value, _ = lax.optimization_barrier((value, self.past[-self.depth]))
        arrived = rotated(value, steps)
        self.past.append(arrived)
        return arrived


def dot(left, right):
    return jnp.dot(left, right, preferred_element_type=f32)


def dot_t(left, right):
    return lax.dot_general(left, right, (((1,), (1,)), ((), ())), preferred_element_type=f32)


def rows_at(matrix, start, size):
    return lax.dynamic_slice_in_dim(matrix, start, size, 0)


def cols_at(matrix, start, size):
    return lax.dynamic_slice_in_dim(matrix, start, size, 1)


def total(terms):
    result = terms[0]
    for term in terms[1:]:
        result = result + term
    return result


def soft_min(first, second):
    return 0.5 * (
        first + second - jnp.sqrt((first - second) * (first - second) + softness * softness)
    )


def soft_max(first, second):
    return 0.5 * (
        first + second + jnp.sqrt((first - second) * (first - second) + softness * softness)
    )


def soft_relu(difference):
    return 0.5 * (difference + jnp.sqrt(difference * difference + softness * softness))


def box_loss(logits, target_box):
    scaled_box = jax.nn.sigmoid(logits) * 1000.0
    centre_x = scaled_box[:, 0]
    centre_y = scaled_box[:, 1]
    box_width = scaled_box[:, 2]
    box_height = scaled_box[:, 3]
    left_pred = centre_x - 0.5 * box_width
    right_pred = centre_x + 0.5 * box_width
    lower_pred = centre_y - 0.5 * box_height
    upper_pred = centre_y + 0.5 * box_height
    target = target_box.astype(f32)
    inner_width = soft_relu(soft_min(right_pred, target[:, 2]) - soft_max(left_pred, target[:, 0]))
    inner_height = soft_relu(
        soft_min(upper_pred, target[:, 3]) - soft_max(lower_pred, target[:, 1])
    )
    intersection_area = inner_width * inner_height
    target_area = (target[:, 2] - target[:, 0]) * (target[:, 3] - target[:, 1])
    union_area = box_width * box_height + target_area - intersection_area
    outer_width = soft_max(right_pred, target[:, 2]) - soft_min(left_pred, target[:, 0])
    outer_height = soft_max(upper_pred, target[:, 3]) - soft_min(lower_pred, target[:, 1])
    enclosing = outer_width * outer_height
    return loss_scale * jnp.mean(
        1.0 - intersection_area / union_area + (enclosing - union_area) / enclosing
    )


def head_rows(pooled, gains, weights, head_bias, target_box, pool_share, full_width):
    highest = lax.Precision.HIGHEST
    square = total([jnp.sum(p * p, axis=1) for p in pooled])
    inverse = lax.rsqrt(square / full_width + epsilon)[:, None]
    projected = inverse * total(
        [
            lax.dot_general(p * g, w, (((1,), (1,)), ((), ())), precision=highest)
            for p, g, w in zip(pooled, gains, weights)
        ]
    )
    loss_value, pullback = jax.vjp(lambda value: box_loss(value, target_box), projected + head_bias)
    logit_grad = pullback(jnp.ones((), f32))[0]
    row_mean = jnp.sum(logit_grad * projected, axis=1, keepdims=True) / full_width
    rows = []
    for p, g, w in zip(pooled, gains, weights):
        pooled_grad = inverse * (
            g * jnp.dot(logit_grad, w, precision=highest) - p * inverse * row_mean
        )
        token_grad = pool_share[:, :, None] * pooled_grad[:, None, :]
        rows.append(token_grad.reshape(-1, p.shape[1]).astype(bf16))
    return rows


def per_device(
    forward_input,
    saved_last,
    saved_first,
    first_cotangent,
    section_entry,
    last_gain,
    last_up,
    last_down,
    first_gain,
    first_up,
    first_down,
    head_gain,
    head_weight,
    head_bias,
    prompt_length,
    keep_mask,
    target_box,
):
    count = lax.axis_size("tensor")
    me = lax.axis_index("tensor")
    section_index = lax.axis_index("section")
    opening = section_index == 0
    closing = section_index == lax.axis_size("section") - 1
    entering, saved, cotangent = forward_input[0], saved_first[0], first_cotangent[0]
    last_up, last_down, first_up, first_down = last_up[0], last_down[0], first_up[0], first_down[0]
    tokens, width = entering.shape
    full_width = width * count
    hidden_width = last_up.shape[1]
    chunk = min(width, chunk_width)
    pieces = range(width // chunk)
    others = range(1, count)
    after = [lax.rem(me + k, count) for k in range(count)]
    before = [lax.rem(me + count - k, count) for k in range(count)]

    def piece(values, j):
        return values[:, j * chunk : (j + 1) * chunk]

    def up_rows(up_matrix, device, j):
        return rows_at(up_matrix, device * width + j * chunk, chunk)

    def down_cols(down_matrix, device, j):
        return cols_at(down_matrix, device * width + j * chunk, chunk)

    def square_sum(values):
        values = values.astype(f32)
        return jnp.sum(values * values, axis=1)

    lane = Lane(2)
    first_gain_cols = rows_at(first_gain[0], me * width, width)
    last_gain_cols = rows_at(last_gain[0], me * width, width)

    def scaled(values, gain_cols):
        return (values.astype(f32) * gain_cols).astype(bf16)

    stored = jnp.where(closing, entering, saved_last[0])

    cotangent_blocks = [cotangent] + [lane.send(cotangent, k) for k in others]
    squares = jnp.stack([square_sum(saved), square_sum(entering), square_sum(stored)])
    squares = total([squares] + [rotated(squares, k) for k in others])
    inverses = lax.rsqrt(squares / full_width + epsilon)
    head_weights = [head_weight.T]
    head_weights += [rotated(head_weight.T, k) for k in others]

    def exchange_up(up_matrix, j):
        return [up_rows(up_matrix, before[0], j)] + [
            lane.send(up_rows(up_matrix, after[k], j), k) for k in others
        ]

    first_up_blocks = [exchange_up(first_up, j) for j in pieces]

    def hidden_parts(normed_pieces, up_blocks):
        return [
            total([dot(normed_pieces[j], up_blocks[j][k]) for j in pieces]) for k in range(count)
        ]

    def collect_hidden(parts):
        return total(
            [parts[0]] + [lane.send(parts[k].astype(bf16), -k).astype(f32) for k in others]
        )

    first_saved_scaled = scaled(saved, first_gain_cols)
    first_saved_parts = hidden_parts(
        [piece(first_saved_scaled, j) for j in pieces], first_up_blocks
    )
    first_act_grad = total(
        [
            dot_t(cotangent_blocks[k], cols_at(first_down, before[k] * width, width))
            for k in range(count)
        ]
    )

    last_up_blocks = [exchange_up(last_up, 0)]
    first_saved_pre = collect_hidden(first_saved_parts) * inverses[0][:, None]
    if len(pieces) > 1:
        last_up_blocks.append(exchange_up(last_up, 1))

    def hidden_grad(pre, act_grad):
        gate = jax.nn.sigmoid(pre)
        pre_grad = (act_grad * gate * (1.0 + pre * (1.0 - gate))).astype(bf16)
        along = jnp.sum(pre_grad.astype(f32) * pre, axis=1)
        blocks = [pre_grad] + [lane.send(pre_grad, k) for k in others]
        along = total([along] + [rotated(along, k) for k in others])
        return blocks, along / full_width

    def input_grad(values, given, inverse, gain_cols, blocks, along, up_blocks, j):
        norm_grad = total([dot_t(blocks[k], up_blocks[j][k]) for k in range(count)])
        unit = values.astype(f32) * inverse[:, None]
        return (
            given.astype(f32)
            + inverse[:, None] * (gain_cols * norm_grad - unit * along[:, None])
        ).astype(bf16)

    first_blocks, first_along = hidden_grad(first_saved_pre, first_act_grad)
    for j in pieces[2:]:
        last_up_blocks.append(exchange_up(last_up, j))

    returned = []
    for j in pieces:
        gradient = input_grad(
            piece(saved, j),
            piece(cotangent, j),
            inverses[0],
            first_gain_cols[j * chunk : (j + 1) * chunk],
            first_blocks,
            first_along,
            first_up_blocks,
            j,
        )
        returned.append(shifted(gradient, "section", -1))

    def send_returned(j):
        return [returned[j]] + [lane.send(returned[j], k) for k in others]

    early = len(pieces) // 2
    returned_blocks = [send_returned(0)] if early else []

    both = jnp.concatenate([scaled(entering, last_gain_cols), scaled(stored, last_gain_cols)], 0)
    both_parts = hidden_parts([piece(both, j) for j in pieces], last_up_blocks)
    both_pre = collect_hidden(both_parts)
    for j in pieces[1:early]:
        returned_blocks.append(send_returned(j))
    forward_pre = both_pre[:tokens] * inverses[1][:, None]
    stored_pre = both_pre[tokens:] * inverses[2][:, None]

    def layer_out(values, activated, down_matrix, j):
        terms = [
            lane.send(dot(activated, down_cols(down_matrix, after[k], j)).astype(bf16), k)
            for k in others
        ]
        mine = dot(activated, down_cols(down_matrix, me, j))
        return (values.astype(f32) + total([mine] + [t.astype(f32) for t in terms])).astype(bf16)

    activated = jax.nn.silu(forward_pre).astype(bf16)
    hidden = [layer_out(piece(entering, j), activated, last_down, j) for j in pieces]
    for j in pieces[early:]:
        returned_blocks.append(send_returned(j))

    entry = [
        jnp.where(opening, piece(section_entry, j), shifted(hidden[j], "section", 1))
        for j in pieces
    ]
    entry_squares = total([square_sum(e) for e in entry])
    entry_squares = total([entry_squares] + [rotated(entry_squares, k) for k in others])
    entry_inverse = lax.rsqrt(entry_squares / full_width + epsilon)
    entry_parts = hidden_parts(
        [
            scaled(entry[j], first_gain_cols[j * chunk : (j + 1) * chunk])
            for j in pieces
        ],
        first_up_blocks,
    )
    entry_pre = collect_hidden(entry_parts) * entry_inverse[:, None]

    row_count = keep_mask.shape[0]
    positions = jnp.arange(keep_mask.shape[1], dtype=jnp.int32)[None, :]
    starts = prompt_length[:, None]
    pool_weights = (positions == starts - 1).astype(f32) + (positions >= starts).astype(
        f32
    ) * keep_mask.astype(f32)
    pool_counts = jnp.sum(pool_weights, axis=1)[:, None]
    pooled = jnp.concatenate(
        [
            jnp.einsum(
                "rt,rtd->rd",
                pool_weights,
                h.astype(f32).reshape(row_count, keep_mask.shape[1], chunk),
                precision=lax.Precision.HIGHEST,
            )
            for h in hidden
        ],
        axis=1,
    ) / pool_counts
    pooled = [pooled] + [rotated(pooled, k) for k in others]
    head_gains = [rows_at(head_gain, before[k] * width, width) for k in range(count)]
    head_grads = head_rows(
        pooled, head_gains, head_weights, head_bias, target_box, pool_weights / pool_counts, full_width
    )

    given = [
        [jnp.where(closing, piece(head_grads[k], j), returned_blocks[j][k]) for k in range(count)]
        for j in pieces
    ]
    last_act_grad = total(
        [
            dot_t(given[j][k], down_cols(last_down, before[k], j))
            for j in pieces
            for k in range(count)
        ]
    )
    last_blocks, last_along = hidden_grad(stored_pre, last_act_grad)

    entry_activated = jax.nn.silu(entry_pre).astype(bf16)
    layer_output = jnp.concatenate(
        [layer_out(entry[j], entry_activated, first_down, j) for j in pieces], axis=1
    )
    input_gradient = jnp.concatenate(
        [
            input_grad(
                piece(stored, j),
                given[j][0],
                inverses[2],
                last_gain_cols[j * chunk : (j + 1) * chunk],
                last_blocks,
                last_along,
                last_up_blocks,
                j,
            )
            for j in pieces
        ],
        axis=1,
    )
    return (layer_output[None], input_gradient[None])


def solution(mesh):
    placed = (
        P("section", None, "tensor"),
        P("section", None, "tensor"),
        P("section", None, "tensor"),
        P("section", None, "tensor"),
        P(None, "tensor"),
        P("section", None),
        P("section", None, "tensor"),
        P("section", "tensor", None),
        P("section", None),
        P("section", None, "tensor"),
        P("section", "tensor", None),
        P(),
        P("tensor", None),
        P(),
        P(),
        P(),
        P(),
    )
    return jax.shard_map(
        per_device,
        mesh=mesh,
        in_specs=placed,
        out_specs=(P("section", None, "tensor"), P("section", None, "tensor")),
        check_vma=False,
    )
```

```python
import functools

import jax
import jax.numpy as jnp
from jax import lax
from jax.experimental import pallas as pl
from jax.experimental.pallas import tpu as pltpu
from jax.sharding import PartitionSpec as P

epsilon = 1e-06
softness = 4.0
loss_scale = 4096.0
chunk_width = 1024

f32 = jnp.float32
bf16 = jnp.bfloat16


def shifted(value, axis, steps):
    count = lax.axis_size(axis)
    initial, last = (max(0, -steps), min(count, count - steps))
    return lax.ppermute(value, axis, [(source, source + steps) for source in range(initial, last)])


def rotated(value, steps):
    count = lax.axis_size("tensor")
    return lax.ppermute(value, "tensor", [(i, (i + steps) % count) for i in range(count)])


def fenced(value, after):
    return lax.optimization_barrier((value, *after))[0] if after else value


def copy_kernel(places, *refs):
    sources, targets, sems = refs[: -len(places) - 1], refs[-len(places) - 1 : -1], refs[-1]
    count, me = lax.axis_size("tensor"), lax.axis_index("tensor")
    copies = []
    for slot, (number, row, column) in enumerate(places):
        rows, columns = targets[slot].shape
        starts = []
        for size, (away, width, offset) in zip((rows, columns), (row, column)):
            start = offset if away is None else lax.rem(me + away, count) * width + offset
            starts.append(pl.ds(start if away is None else pl.multiple_of(start, 128), size))
        source = sources[number].at[starts[0], starts[1]]
        copies.append(pltpu.make_async_copy(source, targets[slot], sems.at[slot]))
    for copy in copies:
        copy.start()
    for copy in copies:
        copy.wait()


here = (None, 0, 0)


def copied(matrices, places, shapes):
    moved = sum(2 * rows * columns for rows, columns in shapes)
    anywhere = pl.BlockSpec(memory_space=pl.ANY)
    return pl.pallas_call(
        functools.partial(copy_kernel, places),
        out_shape=[jax.ShapeDtypeStruct(shape, bf16) for shape in shapes],
        in_specs=[anywhere] * len(matrices),
        out_specs=[pl.BlockSpec(memory_space=pltpu.VMEM)] * len(shapes),
        scratch_shapes=[pltpu.SemaphoreType.DMA((len(shapes),))],
        cost_estimate=pl.CostEstimate(flops=0, bytes_accessed=2 * moved, transcendentals=0),
        compiler_params=pltpu.CompilerParams(vmem_limit_bytes=32 * 1024 * 1024),
        name="copied",
    )(*matrices)


def settled(value):
    return lax.optimization_barrier(value)


def fenced_all(values, after):
    return lax.optimization_barrier((*values, *after))[: len(values)]


class Lane:
    def __init__(self, depth):
        self.depth = depth
        self.past = []

    def send(self, value, steps, after=(), depth=None):
        depth = depth or self.depth
        if len(self.past) >= depth:
            after = (self.past[-depth], *after)
        value = fenced(value, after)
        arrived = rotated(value, steps)
        self.past.append(arrived)
        return arrived


def dot(left, right):
    return jnp.dot(left, right, preferred_element_type=f32)


def dot_t(left, right):
    return lax.dot_general(left, right, (((1,), (1,)), ((), ())), preferred_element_type=f32)


def rows_at(matrix, start, size):
    return lax.dynamic_slice_in_dim(matrix, start, size, 0)


def cols_at(matrix, start, size):
    return lax.dynamic_slice_in_dim(matrix, start, size, 1)


def total(terms):
    result = terms[0]
    for term in terms[1:]:
        result = result + term
    return result


def soft_min(first, second):
    return 0.5 * (
        first + second - jnp.sqrt((first - second) * (first - second) + softness * softness)
    )


def soft_max(first, second):
    return 0.5 * (
        first + second + jnp.sqrt((first - second) * (first - second) + softness * softness)
    )


def soft_relu(difference):
    return 0.5 * (difference + jnp.sqrt(difference * difference + softness * softness))


def box_loss(logits, target):
    centre_x, centre_y, box_width, box_height = [jax.nn.sigmoid(v) * 1000.0 for v in logits]
    left, lower, right, upper = target
    left_pred = centre_x - 0.5 * box_width
    right_pred = centre_x + 0.5 * box_width
    lower_pred = centre_y - 0.5 * box_height
    upper_pred = centre_y + 0.5 * box_height
    inner_width = soft_relu(soft_min(right_pred, right) - soft_max(left_pred, left))
    inner_height = soft_relu(soft_min(upper_pred, upper) - soft_max(lower_pred, lower))
    intersection_area = inner_width * inner_height
    target_area = (right - left) * (upper - lower)
    union_area = box_width * box_height + target_area - intersection_area
    outer_width = soft_max(right_pred, right) - soft_min(left_pred, left)
    outer_height = soft_max(upper_pred, upper) - soft_min(lower_pred, lower)
    enclosing = outer_width * outer_height
    return 1.0 - intersection_area / union_area + (enclosing - union_area) / enclosing


def gate_kernel(count, mine_ref, *refs):
    got_refs, inverse_ref, act_grad_ref = refs[: count - 1], refs[count - 1], refs[count]
    grad_ref, along_ref = refs[count + 1], refs[count + 2]
    tokens = act_grad_ref.shape[0]
    pre = total([mine_ref[...]] + [ref[...].astype(f32) for ref in got_refs]) * inverse_ref[...]
    first = pre[:tokens]
    gate = jax.nn.sigmoid(first)
    grad = (act_grad_ref[...] * gate * (1.0 + first * (1.0 - gate))).astype(bf16)
    grad_ref[...] = grad
    along_ref[...] = lax.dot_general(
        jnp.ones((1, first.shape[1]), f32),
        grad.astype(f32) * first,
        (((1,), (1,)), ((), ())),
        precision=lax.Precision.HIGHEST,
        preferred_element_type=f32,
    )
    if pre.shape[0] > tokens:
        second = pre[tokens:]
        refs[count + 3][...] = (second * jax.nn.sigmoid(second)).astype(bf16)


def gated(mine, got, inverse, act_grad):
    tokens, hidden_width = act_grad.shape
    shapes = [
        jax.ShapeDtypeStruct((tokens, hidden_width), bf16),
        jax.ShapeDtypeStruct((1, tokens), f32),
    ]
    if mine.shape[0] > tokens:
        shapes.append(jax.ShapeDtypeStruct((mine.shape[0] - tokens, hidden_width), bf16))
    whole = pl.BlockSpec(memory_space=pltpu.VMEM)
    return pl.pallas_call(
        functools.partial(gate_kernel, len(got) + 1),
        out_shape=shapes,
        in_specs=[whole] * (len(got) + 3),
        out_specs=[whole] * len(shapes),
        compiler_params=pltpu.CompilerParams(vmem_limit_bytes=32 * 1024 * 1024),
        name="gated",
    )(mine, *got, inverse[:, None], act_grad)


def head_kernel(count, full_width, *refs):
    pooled_refs, gain_refs, weight_refs = (
        refs[:count],
        refs[count : 2 * count],
        refs[2 * count : 3 * count],
    )
    bias_ref, target_ref, counts_ref = refs[3 * count : 3 * count + 3]
    out_refs = refs[3 * count + 3 :]
    rows = pooled_refs[0].shape[0]
    for row in range(rows):
        inverse_count = 1.0 / counts_ref[row : row + 1, :]
        pooled = [ref[row : row + 1, :] * inverse_count for ref in pooled_refs]
        square = total([jnp.sum(p * p, axis=1, keepdims=True) for p in pooled])
        inverse = lax.rsqrt(square / full_width + epsilon)
        projected = inverse * total(
            [
                jnp.sum((p * g[...]) * w[...], axis=1, keepdims=True)
                for p, g, w in zip(pooled, gain_refs, weight_refs)
            ]
        )
        projected = [projected[j : j + 1, :] for j in range(4)]
        target = [target_ref[row : row + 1, j : j + 1] for j in range(4)]
        logits = [projected[j] + bias_ref[j : j + 1, :] for j in range(4)]
        _, pullback = jax.vjp(lambda *values: box_loss(values, target), *logits)
        logit_grad = pullback(jnp.full((1, 1), loss_scale / rows, f32))
        row_mean = total([logit_grad[j] * projected[j] for j in range(4)]) / full_width
        for p, g, w, out in zip(pooled, gain_refs, weight_refs, out_refs):
            scaled_grad = total([logit_grad[j] * w[j : j + 1, :] for j in range(4)])
            out[row : row + 1, :] = (
                inverse * (g[...] * scaled_grad - p * inverse * row_mean) * inverse_count
            )


def head_rows(pooled, gains, weights, head_bias, target_box, pool_counts, full_width):
    count = len(pooled)
    whole = pl.BlockSpec(memory_space=pltpu.VMEM)
    rows = pl.pallas_call(
        functools.partial(head_kernel, count, full_width),
        out_shape=[jax.ShapeDtypeStruct(p.shape, f32) for p in pooled],
        in_specs=[whole] * (3 * count + 3),
        out_specs=[whole] * count,
        name="head",
    )(
        *pooled,
        *gains,
        *weights,
        head_bias,
        target_box,
        pool_counts,
    )
    return [row.astype(bf16) for row in rows]


def per_device(
    forward_input,
    saved_last,
    saved_first,
    first_cotangent,
    section_entry,
    last_gain,
    last_up,
    last_down,
    first_gain,
    first_up,
    first_down,
    head_gain,
    head_weight,
    head_bias,
    prompt_length,
    keep_mask,
    target_box,
):
    count = lax.axis_size("tensor")
    me = lax.axis_index("tensor")
    section_index = lax.axis_index("section")
    opening = section_index == 0
    closing = section_index == lax.axis_size("section") - 1
    entering, saved, cotangent = forward_input[0], saved_first[0], first_cotangent[0]
    last_up, last_down, first_up, first_down = last_up[0], last_down[0], first_up[0], first_down[0]
    tokens, width = entering.shape
    full_width = width * count
    hidden_width = last_up.shape[1]
    chunk = min(width, chunk_width)
    pieces = range(width // chunk)
    final = pieces[-1]
    others = range(1, count)
    after = [lax.rem(me + k, count) for k in range(count)]
    before = [lax.rem(me + count - k, count) for k in range(count)]

    def piece(values, j):
        return values[:, j * chunk : (j + 1) * chunk]

    def square_sum(values):
        values = values.astype(f32)
        return jnp.sum(values * values, axis=1)

    lane = Lane(2)
    first_gain_cols = rows_at(first_gain[0], me * width, width)
    last_gain_cols = rows_at(last_gain[0], me * width, width)

    def scaled(values, gain_cols):
        return (values.astype(f32) * gain_cols).astype(bf16)

    def gain_piece(gain_cols, j):
        return gain_cols[j * chunk : (j + 1) * chunk]

    def up_parts(up_matrix, sizes):
        starts = [sum(sizes[:cut]) for cut in range(len(sizes))]
        places = [(0, (k, width, start), here) for start in starts for k in others]
        shapes = [(size, hidden_width) for size in sizes for k in others]
        places.append((0, (0, width, 0), here))
        shapes.append((width, hidden_width))
        parts = copied([up_matrix], places, shapes)
        step = count - 1
        return [parts[i * step : (i + 1) * step] for i in range(len(sizes))], parts[-1]

    def down_parts(down_matrix):
        places = [(0, here, (k, width, 0)) for k in range(count)]
        return copied([down_matrix], places, [(hidden_width, width)] * count)

    def send_up(parts, ahead=(), depth=None):
        return [lane.send(part, k, ahead, depth) for part, k in zip(parts, others)]

    def up_rows(own, got, start, size):
        blocks = [own[start : start + size]]
        for cuts in zip(*got):
            taken, at = [], 0
            for cut in cuts:
                low, high = max(start - at, 0), min(start + size - at, cut.shape[0])
                if low < high:
                    taken.append(cut[low:high])
                at += cut.shape[0]
            blocks.append(taken[0] if len(taken) == 1 else jnp.concatenate(taken, axis=0))
        return blocks

    def exchange_cols(values, ahead=()):
        return [values] + [lane.send(values, k, ahead) for k in others]

    def sum_small(values):
        return total([values] + [rotated(values, k) for k in others])

    def collect(sent):
        return [lane.send(t, -k) for t, k in zip(sent, others)]

    def exchange_grad(pre_grad, along):
        blocks = [pre_grad] + [lane.send(pre_grad, k) for k in others]
        return blocks, sum_small(along)[0] / full_width

    def other_products(normed, got):
        sums = []
        for cuts in zip(*got):
            terms, at = [], 0
            for cut in cuts:
                terms.append(dot(normed[:, at : at + cut.shape[0]], cut))
                at += cut.shape[0]
            early = settled(total(terms[:-1]))
            sums.append((early + terms[-1]).astype(bf16))
        return sums

    def input_grad(values, given, inverse, gain_cols, blocks, along, up_blocks):
        norm_grad = total([dot_t(blocks[k], up_blocks[k]) for k in range(count)])
        unit = values.astype(f32) * inverse[:, None]
        return (
            given.astype(f32)
            + inverse[:, None] * (gain_cols * norm_grad - unit * along[:, None])
        ).astype(bf16)

    def send_out(activated, downs, j, ahead=()):
        values = [dot(activated, piece(downs[k], j)).astype(bf16) for k in others]
        return [lane.send(value, k, ahead) for value, k in zip(values, others)]

    def add_out(values, mine, terms):
        return (values.astype(f32) + total([mine] + [t.astype(f32) for t in terms])).astype(bf16)

    def act_grad_terms(blocks, downs):
        return [dot_t(blocks[k], downs[-k]) for k in range(count)]

    stored = jnp.where(closing, entering, saved_last[0])

    last_parts, last_up_own = up_parts(last_up, [width // 2] * 2)
    cotangents = exchange_cols(cotangent)
    last_got = [send_up(last_parts[0])]
    last_downs = down_parts(last_down)
    first_parts, first_up_own = up_parts(first_up, [width // 4, width // 4, width // 2])
    first_downs = down_parts(first_down)
    squares = jnp.stack([square_sum(saved), square_sum(entering), square_sum(stored)])
    head_gains = [rows_at(head_gain, before[k] * width, width)[None, :] for k in range(count)]
    head_small = [head_weight.T, head_bias[:, None], target_box.astype(f32)]
    entering_scaled = scaled(entering, last_gain_cols)
    stored_scaled = scaled(stored, last_gain_cols)
    first_saved = scaled(saved, first_gain_cols)

    last_got.append(send_up(last_parts[1]))
    ahead = [
        *last_downs, first_up_own, *first_downs, squares, *head_gains, *head_small, entering_scaled,
        stored_scaled, first_saved,
    ]
    first_got = [send_up(first_parts[0], ahead)]
    sent = other_products(entering_scaled, last_got)
    mine = dot(fenced(entering_scaled, sent), last_up_own)
    got = collect(sent)
    squares = fenced(squares, sent)
    squares = total([squares] + [rotated(squares, k) for k in others])
    inverses = lax.rsqrt(squares / full_width + epsilon)
    head_weights = [head_small[0]] + [rotated(fenced(head_small[0], sent), k) for k in others]
    act_grad = total(act_grad_terms(cotangents, first_downs))
    first_got.append(send_up(first_parts[1], sent))
    stored_sent = other_products(fenced(stored_scaled, sent), last_got)
    stored_mine = dot(fenced(stored_scaled, sent), last_up_own)
    got = fenced_all(got, [*stored_sent, stored_mine, act_grad])
    entering_pre = total([mine] + [t.astype(f32) for t in got]) * inverses[1][:, None]

    activated = jax.nn.silu(entering_pre).astype(bf16)
    gots = [send_out(activated, last_downs, j) for j in pieces[:-1]]
    mine = dot(activated, last_downs[0])
    gots.append(send_out(activated, last_downs, final, [mine]))
    first_got.append(send_up(first_parts[2], depth=3))
    hidden = add_out(entering, mine, [jnp.concatenate(t, axis=1) for t in zip(*gots)])
    entry = jnp.where(opening, section_entry, shifted(hidden, "section", 1))

    row_count, row_length = keep_mask.shape
    positions = jnp.arange(row_length, dtype=jnp.int32)[None, :]
    starts = prompt_length[:, None]
    pool_weights = (positions == starts - 1).astype(f32) + (positions >= starts).astype(
        f32
    ) * keep_mask.astype(f32)
    pool_counts = jnp.sum(pool_weights, axis=1)[:, None]

    def pool(values):
        if row_count == 1:
            return dot(pool_weights.astype(bf16), values)
        values = values.reshape(row_count, row_length, values.shape[1])
        return jnp.einsum(
            "rt,rtd->rd", pool_weights.astype(bf16), values, preferred_element_type=f32
        )

    def on_tokens(rows):
        values = pool_weights[:, :, None] * rows.astype(f32)[:, None, :]
        return values.reshape(tokens, rows.shape[1])

    pooled = pool(fenced(hidden, [entry]))
    pooled = [pooled] + [rotated(pooled, k) for k in others]
    head_grads = head_rows(
        pooled, head_gains, head_weights, *head_small[1:], pool_counts, full_width
    )
    head_act_grad = total([dot_t(head_grads[k], last_downs[-k]) for k in range(count)])

    entry_squares = sum_small(square_sum(entry))
    entry_inverse = lax.rsqrt(entry_squares / full_width + epsilon)
    pair = jnp.concatenate([first_saved, scaled(entry, first_gain_cols)], axis=0)
    sent = other_products(pair, first_got)
    mine = dot(fenced(pair, sent), first_up_own)
    got = collect(sent)
    stored_got = collect(fenced_all(stored_sent, sent))

    pair_inverse = jnp.concatenate([inverses[0], entry_inverse])
    pre_grad, along, entry_activated = gated(mine, got, pair_inverse, act_grad)
    first_blocks, first_along = exchange_grad(pre_grad, along)
    early = (len(pieces) + 1) // 2

    def first_out(low, high):
        columns = slice(low * chunk, high * chunk)
        values = [dot(entry_activated, first_downs[k][:, columns]).astype(bf16) for k in others]
        return [lane.send(value, k) for value, k in zip(values, others)]

    gots = [first_out(0, early)]
    returned = []
    for j in pieces:
        gradient = input_grad(
            piece(saved, j),
            piece(cotangent, j),
            inverses[0],
            gain_piece(first_gain_cols, j),
            fenced_all(first_blocks, returned[-1:]),
            first_along,
            up_rows(first_up_own, first_got, j * chunk, chunk),
        )
        returned.append(gradient)
    returned = [shifted(gradient, "section", -1) for gradient in returned]

    act_grads = []
    for j in pieces:
        ahead = act_grads[j - 2 : j - 1] if j > 1 else ()
        if j == final and early < final:
            gots.append(first_out(early, final))
            ahead = [*ahead, *gots[-1]]
        blocks = exchange_cols(returned[j], ahead)
        terms = act_grad_terms(blocks, [piece(d, j) for d in last_downs])
        act_grads.append(total(act_grads[-1:] + terms))
    last_act_grad = jnp.where(closing, on_tokens(head_act_grad), act_grads[-1])
    pre_grad, along = gated(stored_mine, stored_got, inverses[2], last_act_grad)
    last_blocks, last_along = exchange_grad(pre_grad, along)
    if early <= final:
        gots.append(first_out(max(early, final), len(pieces)))
    outs, at = [], 0
    for got in gots:
        columns = slice(at, at + got[0].shape[1])
        mine = dot(entry_activated, first_downs[0][:, columns])
        outs.append(add_out(entry[:, columns], mine, got))
        at = columns.stop
    layer_output = jnp.concatenate(outs, axis=1)
    given = [
        jnp.where(closing, on_tokens(piece(head_grads[0], j)).astype(bf16), returned[j])
        for j in pieces
    ]
    input_gradient = jnp.concatenate(
        [
            input_grad(
                piece(stored, j),
                given[j],
                inverses[2],
                gain_piece(last_gain_cols, j),
                last_blocks,
                last_along,
                up_rows(last_up_own, last_got, j * chunk, chunk),
            )
            for j in pieces
        ],
        axis=1,
    )
    return (layer_output[None], input_gradient[None])


def solution(mesh):
    placed = (
        P("section", None, "tensor"),
        P("section", None, "tensor"),
        P("section", None, "tensor"),
        P("section", None, "tensor"),
        P(None, "tensor"),
        P("section", None),
        P("section", None, "tensor"),
        P("section", "tensor", None),
        P("section", None),
        P("section", None, "tensor"),
        P("section", "tensor", None),
        P(),
        P("tensor", None),
        P(),
        P(),
        P(),
        P(),
    )
    return jax.shard_map(
        per_device,
        mesh=mesh,
        in_specs=placed,
        out_specs=(P("section", None, "tensor"), P("section", None, "tensor")),
        check_vma=False,
    )
```

```python
import functools

import jax
import jax.numpy as jnp
from jax import lax
from jax.experimental import pallas as pl
from jax.experimental.pallas import tpu as pltpu
from jax.sharding import PartitionSpec as P

epsilon = 1e-06
softness = 4.0
loss_scale = 4096.0
chunk_width = 1024

f32 = jnp.float32
bf16 = jnp.bfloat16


def shifted(value, axis, steps):
    count = lax.axis_size(axis)
    initial, last = (max(0, -steps), min(count, count - steps))
    return lax.ppermute(value, axis, [(source, source + steps) for source in range(initial, last)])


def rotated(value, steps):
    count = lax.axis_size("tensor")
    return lax.ppermute(value, "tensor", [(i, (i + steps) % count) for i in range(count)])


def fenced(value, after):
    return lax.optimization_barrier((value, *after))[0] if after else value


def copy_kernel(places, *refs):
    sources, targets, sems = refs[: -len(places) - 1], refs[-len(places) - 1 : -1], refs[-1]
    count, me = lax.axis_size("tensor"), lax.axis_index("tensor")
    copies = []
    for slot, (number, row, column) in enumerate(places):
        rows, columns = targets[slot].shape
        starts = []
        for size, (away, width, offset) in zip((rows, columns), (row, column)):
            start = offset if away is None else lax.rem(me + away, count) * width + offset
            starts.append(pl.ds(start if away is None else pl.multiple_of(start, 128), size))
        source = sources[number].at[starts[0], starts[1]]
        copies.append(pltpu.make_async_copy(source, targets[slot], sems.at[slot]))
    for copy in copies:
        copy.start()
    for copy in copies:
        copy.wait()


here = (None, 0, 0)


def copied(matrices, places, shapes):
    moved = sum(2 * rows * columns for rows, columns in shapes)
    anywhere = pl.BlockSpec(memory_space=pl.ANY)
    return pl.pallas_call(
        functools.partial(copy_kernel, places),
        out_shape=[jax.ShapeDtypeStruct(shape, bf16) for shape in shapes],
        in_specs=[anywhere] * len(matrices),
        out_specs=[pl.BlockSpec(memory_space=pltpu.VMEM)] * len(shapes),
        scratch_shapes=[pltpu.SemaphoreType.DMA((len(shapes),))],
        cost_estimate=pl.CostEstimate(flops=0, bytes_accessed=2 * moved, transcendentals=0),
        compiler_params=pltpu.CompilerParams(vmem_limit_bytes=32 * 1024 * 1024),
        name="copied",
    )(*matrices)


def settled(value):
    return lax.optimization_barrier(value)


def fenced_all(values, after):
    return lax.optimization_barrier((*values, *after))[: len(values)]


class Lane:
    def __init__(self, depth):
        self.depth = depth
        self.past = []

    def send(self, value, steps, after=(), depth=None):
        depth = depth or self.depth
        if len(self.past) >= depth:
            after = (self.past[-depth], *after)
        value = fenced(value, after)
        arrived = rotated(value, steps)
        self.past.append(arrived)
        return arrived


def dot(left, right):
    return jnp.dot(left, right, preferred_element_type=f32)


def dot_t(left, right):
    return lax.dot_general(left, right, (((1,), (1,)), ((), ())), preferred_element_type=f32)


def rows_at(matrix, start, size):
    return lax.dynamic_slice_in_dim(matrix, start, size, 0)


def cols_at(matrix, start, size):
    return lax.dynamic_slice_in_dim(matrix, start, size, 1)


def total(terms):
    result = terms[0]
    for term in terms[1:]:
        result = result + term
    return result


def soft_min(first, second):
    return 0.5 * (
        first + second - jnp.sqrt((first - second) * (first - second) + softness * softness)
    )


def soft_max(first, second):
    return 0.5 * (
        first + second + jnp.sqrt((first - second) * (first - second) + softness * softness)
    )


def soft_relu(difference):
    return 0.5 * (difference + jnp.sqrt(difference * difference + softness * softness))


def box_loss(logits, target):
    centre_x, centre_y, box_width, box_height = [jax.nn.sigmoid(v) * 1000.0 for v in logits]
    left, lower, right, upper = target
    left_pred = centre_x - 0.5 * box_width
    right_pred = centre_x + 0.5 * box_width
    lower_pred = centre_y - 0.5 * box_height
    upper_pred = centre_y + 0.5 * box_height
    inner_width = soft_relu(soft_min(right_pred, right) - soft_max(left_pred, left))
    inner_height = soft_relu(soft_min(upper_pred, upper) - soft_max(lower_pred, lower))
    intersection_area = inner_width * inner_height
    target_area = (right - left) * (upper - lower)
    union_area = box_width * box_height + target_area - intersection_area
    outer_width = soft_max(right_pred, right) - soft_min(left_pred, left)
    outer_height = soft_max(upper_pred, upper) - soft_min(lower_pred, lower)
    enclosing = outer_width * outer_height
    return 1.0 - intersection_area / union_area + (enclosing - union_area) / enclosing


def column(row):
    return jnp.transpose(jnp.broadcast_to(row, (128, row.shape[1])))[:, :1]


def gate_kernel(count, pairs, mine_ref, act_grad_ref, *refs):
    got_refs, refs = refs[: count - 1], refs[count - 1 :]
    left_refs, right_refs, refs = refs[:pairs], refs[pairs : 2 * pairs], refs[2 * pairs :]
    groups = mine_ref.shape[0] // act_grad_ref.shape[0]
    inverse_refs, (grad_ref, along_ref, *out_refs) = refs[:groups], refs[groups:]
    tokens = act_grad_ref.shape[0]
    pre = total([mine_ref[...]] + [ref[...].astype(f32) for ref in got_refs])
    first = pre[:tokens] * column(inverse_refs[0][...])
    gate = jax.nn.sigmoid(first)
    act_grad = total(
        [act_grad_ref[...]] + [dot_t(x[...], w[...]) for x, w in zip(left_refs, right_refs)]
    )
    grad = (act_grad * gate * (1.0 + first * (1.0 - gate))).astype(bf16)
    grad_ref[...] = grad
    along_ref[...] = lax.dot_general(
        jnp.ones((1, first.shape[1]), f32),
        grad.astype(f32) * first,
        (((1,), (1,)), ((), ())),
        precision=lax.Precision.HIGHEST,
        preferred_element_type=f32,
    )
    if groups > 1:
        second = pre[tokens:] * column(inverse_refs[1][...])
        out_refs[0][...] = (second * jax.nn.sigmoid(second)).astype(bf16)


def gated(mine, got, inverses, act_grad, left=(), right=()):
    tokens, hidden_width = act_grad.shape
    shapes = [
        jax.ShapeDtypeStruct((tokens, hidden_width), bf16),
        jax.ShapeDtypeStruct((1, tokens), f32),
    ]
    if mine.shape[0] > tokens:
        shapes.append(jax.ShapeDtypeStruct((mine.shape[0] - tokens, hidden_width), bf16))
    whole = pl.BlockSpec(memory_space=pltpu.VMEM)
    return pl.pallas_call(
        functools.partial(gate_kernel, len(got) + 1, len(left)),
        out_shape=shapes,
        in_specs=[whole] * (len(got) + 2 + 2 * len(left) + len(inverses)),
        out_specs=[whole] * len(shapes),
        compiler_params=pltpu.CompilerParams(vmem_limit_bytes=32 * 1024 * 1024),
        name="gated",
    )(mine, act_grad, *got, *left, *right, *inverses)


def head_kernel(count, full_width, *refs):
    pooled_refs, weight_refs = refs[:count], refs[count : 2 * count]
    gain_ref, bias_ref, target_ref, prompt_ref, keep_ref = refs[2 * count : 2 * count + 5]
    out_refs = refs[2 * count + 5 :]
    me = lax.axis_index("tensor")
    rows, width = pooled_refs[0].shape
    gains = []
    for k in range(count):
        start = pl.multiple_of(lax.rem(me + count - k, count) * width, width)
        gains.append(gain_ref[:, pl.ds(start, width)])
    for row in range(rows):
        weights = pool_weights(prompt_ref[row], keep_ref[row : row + 1, :])
        inverse_count = 1.0 / jnp.sum(weights, axis=1, keepdims=True)
        pooled = [ref[row : row + 1, :] * inverse_count for ref in pooled_refs]
        square = total([jnp.sum(p * p, axis=1, keepdims=True) for p in pooled])
        inverse = lax.rsqrt(square / full_width + epsilon)
        projected = inverse * total(
            [
                jnp.sum((p * g) * w[...], axis=1, keepdims=True)
                for p, g, w in zip(pooled, gains, weight_refs)
            ]
        )
        projected = [projected[j : j + 1, :] for j in range(4)]
        target = [target_ref[row, j].astype(f32) for j in range(4)]
        logits = [projected[j] + bias_ref[j] for j in range(4)]
        _, pullback = jax.vjp(lambda *values: box_loss(values, target), *logits)
        logit_grad = pullback(jnp.full((1, 1), loss_scale / rows, f32))
        row_mean = total([logit_grad[j] * projected[j] for j in range(4)]) / full_width
        for p, g, w, out in zip(pooled, gains, weight_refs, out_refs):
            scaled_grad = total([logit_grad[j] * w[j : j + 1, :] for j in range(4)])
            out[row : row + 1, :] = (
                inverse * (g * scaled_grad - p * inverse * row_mean) * inverse_count
            )


def pool_weights(prompt_length, keep_row):
    positions = lax.broadcasted_iota(jnp.int32, keep_row.shape, 1)
    starting = jnp.where(positions == prompt_length - 1, 1.0, 0.0)
    kept = jnp.where(positions >= prompt_length, 1.0, 0.0)
    return starting + kept * keep_row.astype(f32)


def head_rows(pooled, weights, head_gain, head_bias, target_box, prompt_length, keep_mask, full_width):
    count = len(pooled)
    whole = pl.BlockSpec(memory_space=pltpu.VMEM)
    scalars = pl.BlockSpec(memory_space=pltpu.SMEM)
    rows = pl.pallas_call(
        functools.partial(head_kernel, count, full_width),
        out_shape=[jax.ShapeDtypeStruct(p.shape, f32) for p in pooled],
        in_specs=[whole] * (2 * count + 1) + [scalars] * 3 + [whole],
        out_specs=[whole] * count,
        name="head",
    )(*pooled, *weights, head_gain[None, :], head_bias, target_box, prompt_length, keep_mask)
    return [row.astype(bf16) for row in rows]


def per_device(
    forward_input,
    saved_last,
    saved_first,
    first_cotangent,
    section_entry,
    last_gain,
    last_up,
    last_down,
    first_gain,
    first_up,
    first_down,
    head_gain,
    head_weight,
    head_bias,
    prompt_length,
    keep_mask,
    target_box,
):
    count = lax.axis_size("tensor")
    me = lax.axis_index("tensor")
    section_index = lax.axis_index("section")
    opening = section_index == 0
    closing = section_index == lax.axis_size("section") - 1
    entering, saved, cotangent = forward_input[0], saved_first[0], first_cotangent[0]
    last_up, last_down, first_up, first_down = last_up[0], last_down[0], first_up[0], first_down[0]
    tokens, width = entering.shape
    full_width = width * count
    hidden_width = last_up.shape[1]
    chunk = min(width, chunk_width)
    pieces = range(width // chunk)
    final = pieces[-1]
    others = range(1, count)
    after = [lax.rem(me + k, count) for k in range(count)]
    before = [lax.rem(me + count - k, count) for k in range(count)]

    def piece(values, j):
        return values[:, j * chunk : (j + 1) * chunk]

    def square_sum(values):
        values = values.astype(f32)
        return jnp.sum(values * values, axis=1)

    lane = Lane(2)
    first_gain_cols = rows_at(first_gain[0], me * width, width)
    last_gain_cols = rows_at(last_gain[0], me * width, width)

    def scaled(values, gain_cols):
        return (values.astype(f32) * gain_cols).astype(bf16)

    def gain_piece(gain_cols, j):
        return gain_cols[j * chunk : (j + 1) * chunk]

    def up_parts(up_matrix, sizes):
        starts = [sum(sizes[:cut]) for cut in range(len(sizes))]
        places = [(0, (k, width, start), here) for start in starts for k in others]
        shapes = [(size, hidden_width) for size in sizes for k in others]
        places.append((0, (0, width, 0), here))
        shapes.append((width, hidden_width))
        parts = copied([up_matrix], places, shapes)
        step = count - 1
        return [parts[i * step : (i + 1) * step] for i in range(len(sizes))], parts[-1]

    def down_parts(down_matrix):
        places = [(0, here, (k, width, 0)) for k in range(count)]
        return copied([down_matrix], places, [(hidden_width, width)] * count)

    def send_up(parts, ahead=(), depth=None):
        return [lane.send(part, k, ahead, depth) for part, k in zip(parts, others)]

    def up_rows(own, got, start, size):
        blocks = [own[start : start + size]]
        for cuts in zip(*got):
            taken, at = [], 0
            for cut in cuts:
                low, high = max(start - at, 0), min(start + size - at, cut.shape[0])
                if low < high:
                    taken.append(cut[low:high])
                at += cut.shape[0]
            blocks.append(taken[0] if len(taken) == 1 else jnp.concatenate(taken, axis=0))
        return blocks

    def exchange_cols(values, ahead=()):
        return [values] + [lane.send(values, k, ahead) for k in others]

    def sum_small(values):
        return total([values] + [rotated(values, k) for k in others])

    def collect(sent):
        return [lane.send(t, -k) for t, k in zip(sent, others)]

    def exchange_grad(pre_grad, along):
        blocks = [pre_grad] + [lane.send(pre_grad, k) for k in others]
        return blocks, sum_small(along)[0] / full_width

    def other_products(normed, got, after=()):
        sums = []
        for cuts in zip(*got):
            terms, at = [], 0
            for cut in cuts[:-1]:
                terms.append(dot(normed[:, at : at + cut.shape[0]], cut))
                at += cut.shape[0]
            early = [settled(total(terms))] if terms else []
            last = dot(fenced(normed[:, at:], [*early, *after]), cuts[-1])
            sums.append(total([*early, last]).astype(bf16))
        return sums

    def input_grad(values, given, inverse, gain_cols, blocks, along, up_blocks):
        norm_grad = total([dot_t(blocks[k], up_blocks[k]) for k in range(count)])
        unit = values.astype(f32) * inverse[:, None]
        return (
            given.astype(f32)
            + inverse[:, None] * (gain_cols * norm_grad - unit * along[:, None])
        ).astype(bf16)

    def send_out(activated, downs, j, ahead=()):
        values = [dot(activated, piece(downs[k], j)).astype(bf16) for k in others]
        return [lane.send(value, k, ahead) for value, k in zip(values, others)]

    def add_out(values, mine, terms):
        return (values.astype(f32) + total([mine] + [t.astype(f32) for t in terms])).astype(bf16)

    def act_grad_terms(blocks, downs):
        return [dot_t(blocks[k], downs[-k]) for k in range(count)]

    stored = jnp.where(closing, entering, saved_last[0])

    last_parts, last_up_own = up_parts(last_up, [width // 2] * 2)
    cotangents = exchange_cols(cotangent)
    last_got = [send_up(last_parts[0])]
    last_downs = down_parts(last_down)
    first_parts, first_up_own = up_parts(first_up, [width // 4, width // 4, width // 2])
    first_downs = down_parts(first_down)
    squares = jnp.stack([square_sum(saved), square_sum(entering), square_sum(stored)])
    head_weights = [head_weight.T]
    entering_scaled = scaled(entering, last_gain_cols)
    stored_scaled = scaled(stored, last_gain_cols)
    first_saved = scaled(saved, first_gain_cols)

    last_got.append(send_up(last_parts[1]))
    ahead = [
        *last_downs, first_up_own, *first_downs, squares, *head_weights, entering_scaled,
        stored_scaled, first_saved,
    ]
    first_got = [send_up(first_parts[0], ahead)]
    sent = other_products(entering_scaled, last_got)
    mine = dot(fenced(entering_scaled, sent), last_up_own)
    got = collect(sent)
    squares = fenced(squares, sent)
    squares = total([squares] + [rotated(squares, k) for k in others])
    inverses = lax.rsqrt(squares / full_width + epsilon)
    head_weights += [rotated(fenced(head_weights[0], sent), k) for k in others]
    act_grad = total(act_grad_terms(cotangents, first_downs))
    first_got.append(send_up(first_parts[1], sent))
    stored_sent = other_products(fenced(stored_scaled, sent), last_got)
    stored_mine = dot(fenced(stored_scaled, sent), last_up_own)
    stored_got = collect(stored_sent)
    inverse_rows = [settled(inverses[i : i + 1]) for i in range(3)]
    first_gains = [settled(gain_piece(first_gain_cols, j)) for j in pieces]
    last_up_got = [settled(jnp.concatenate(cuts, axis=0)) for cuts in zip(*last_got)]
    right = [settled(piece(last_downs[-k], final)) for k in others]
    got = fenced_all(got, [*right, *last_up_got, *stored_sent, stored_mine, act_grad, *inverse_rows, *first_gains, last_gain_cols, *head_weights[1:]])
    entering_pre = total([mine] + [t.astype(f32) for t in got]) * inverses[1][:, None]

    activated = jax.nn.silu(entering_pre).astype(bf16)
    gots = [send_out(activated, last_downs, j) for j in pieces[:-1]]
    mine = dot(activated, last_downs[0])
    gots.append(send_out(activated, last_downs, final, [mine]))
    first_got.append(send_up(first_parts[2], depth=3))
    hidden = add_out(entering, mine, [jnp.concatenate(t, axis=1) for t in zip(*gots)])
    entry = jnp.where(opening, section_entry, shifted(hidden, "section", 1))

    row_count, row_length = keep_mask.shape
    token_weights = jnp.concatenate(
        [pool_weights(prompt_length[row], keep_mask[row : row + 1]) for row in range(row_count)], 0
    )

    def pool(values):
        weights = token_weights.astype(bf16)
        if row_count == 1:
            return dot(weights, values)
        values = values.reshape(row_count, row_length, values.shape[1])
        return jnp.einsum("rt,rtd->rd", weights, values, preferred_element_type=f32)

    def on_tokens(rows):
        values = token_weights[:, :, None] * rows.astype(f32)[:, None, :]
        return values.reshape(tokens, rows.shape[1])

    pooled = pool(fenced(hidden, [entry]))
    pooled = [pooled] + [rotated(pooled, k) for k in others]

    entry_squares = sum_small(square_sum(entry)[None, :])
    entry_inverse = settled(lax.rsqrt(entry_squares / full_width + epsilon))
    pair = jnp.concatenate([first_saved, scaled(entry, first_gain_cols)], axis=0)
    sent = other_products(pair, first_got, [entry_inverse])
    mine = dot(fenced(pair, sent), first_up_own)
    got = collect(sent)

    pre_grad, along, entry_activated = gated(mine, got, [inverse_rows[0], entry_inverse], act_grad)
    first_blocks, first_along = exchange_grad(pre_grad, along)
    early = (len(pieces) + 1) // 2

    def first_out(low, high, activated):
        columns = slice(low * chunk, high * chunk)
        values = [dot(activated, first_downs[k][:, columns]).astype(bf16) for k in others]
        return [lane.send(value, k) for value, k in zip(values, others)]

    gots = [first_out(0, early, entry_activated)]
    returned = []
    for j in pieces:
        gradient = input_grad(
            piece(saved, j),
            piece(cotangent, j),
            inverses[0],
            first_gains[j],
            fenced_all(first_blocks, returned[-1:]),
            first_along,
            up_rows(first_up_own, first_got, j * chunk, chunk),
        )
        returned.append(gradient)
    returned = [shifted(gradient, "section", -1) for gradient in returned]

    act_grads = []
    for j in pieces[:-1]:
        ahead = act_grads[j - 2 : j - 1] if j > 1 else ()
        blocks = exchange_cols(returned[j], ahead)
        terms = act_grad_terms(blocks, [piece(d, j) for d in last_downs])
        act_grads.append(total(act_grads[-1:] + terms))
        if j == 0:
            late = blocks[1:]
    if final == 0:
        late = first_blocks[1:]
    head_grads = head_rows(
        fenced_all(pooled, late),
        head_weights,
        head_gain,
        head_bias,
        target_box,
        prompt_length,
        keep_mask,
        full_width,
    )
    head_act_grad = total([dot_t(head_grads[k], last_downs[-k]) for k in range(count)])
    given = settled(
        jnp.where(
            closing, on_tokens(head_grads[0]).astype(bf16), jnp.concatenate(returned, axis=1)
        )
    )
    act_grad = settled(
        total(
            [
                jnp.where(closing, on_tokens(head_act_grad), 0.0),
                dot_t(returned[-1], piece(last_downs[0], final)),
                *act_grads[-1:],
            ]
        )
    )
    activated_late = fenced(entry_activated, late)
    if early < final:
        gots.append(first_out(early, final, activated_late))
    ahead = [given, act_grad, *right, *(gots[-1] if early < final else ())]
    left = exchange_cols(returned[-1], ahead)[1:]
    pre_grad, along = gated(stored_mine, stored_got, inverse_rows[2:], act_grad, left, right)
    last_blocks, last_along = exchange_grad(pre_grad, along)
    if early <= final:
        gots.append(first_out(max(early, final), len(pieces), activated_late))
    outs, at = [], 0
    for got in gots[:-1]:
        columns = slice(at, at + got[0].shape[1])
        mine = dot(activated_late, first_downs[0][:, columns])
        outs.append(add_out(entry[:, columns], mine, got))
        at = columns.stop
    mine = settled(dot(activated_late, first_downs[0][:, at:]))
    outs = jnp.concatenate([*outs, entry[:, at:]], axis=1)
    got = fenced_all(gots[-1], [mine, outs])
    layer_output = lax.dynamic_update_slice_in_dim(outs, add_out(entry[:, at:], mine, got), at, 1)

    own = settled(dot_t(last_blocks[0], last_up_own))
    norm_grad = total(
        [own] + [dot_t(block, got) for block, got in zip(last_blocks[1:], last_up_got)]
    )
    unit = stored.astype(f32) * inverses[2][:, None]
    input_gradient = (
        given.astype(f32)
        + inverses[2][:, None] * (last_gain_cols * norm_grad - unit * last_along[:, None])
    ).astype(bf16)
    return (layer_output[None], input_gradient[None])


def solution(mesh):
    placed = (
        P("section", None, "tensor"),
        P("section", None, "tensor"),
        P("section", None, "tensor"),
        P("section", None, "tensor"),
        P(None, "tensor"),
        P("section", None),
        P("section", None, "tensor"),
        P("section", "tensor", None),
        P("section", None),
        P("section", None, "tensor"),
        P("section", "tensor", None),
        P(),
        P("tensor", None),
        P(),
        P(),
        P(),
        P(),
    )
    return jax.shard_map(
        per_device,
        mesh=mesh,
        in_specs=placed,
        out_specs=(P("section", None, "tensor"), P("section", None, "tensor")),
        check_vma=False,
    )
```

```python
import functools

import jax
import jax.numpy as jnp
from jax import lax
from jax.experimental import pallas as pl
from jax.experimental.pallas import tpu as pltpu
from jax.sharding import PartitionSpec as P

epsilon = 1e-06
softness = 4.0
loss_scale = 4096.0
chunk_width = 1024

f32 = jnp.float32
bf16 = jnp.bfloat16


def shifted(value, axis, steps):
    count = lax.axis_size(axis)
    initial, last = (max(0, -steps), min(count, count - steps))
    return lax.ppermute(value, axis, [(source, source + steps) for source in range(initial, last)])


def rotated(value, steps):
    count = lax.axis_size("tensor")
    return lax.ppermute(value, "tensor", [(i, (i + steps) % count) for i in range(count)])


def fenced(value, after):
    return lax.optimization_barrier((value, *after))[0] if after else value


def copy_kernel(places, *refs):
    sources, targets, sems = refs[: -len(places) - 1], refs[-len(places) - 1 : -1], refs[-1]
    count, me = lax.axis_size("tensor"), lax.axis_index("tensor")
    copies = []
    for slot, (number, row, column) in enumerate(places):
        rows, columns = targets[slot].shape
        starts = []
        for size, (away, width, offset) in zip((rows, columns), (row, column)):
            start = offset if away is None else lax.rem(me + away, count) * width + offset
            starts.append(pl.ds(start if away is None else pl.multiple_of(start, 128), size))
        source = sources[number].at[starts[0], starts[1]]
        copies.append(pltpu.make_async_copy(source, targets[slot], sems.at[slot]))
    for copy in copies:
        copy.start()
    for copy in copies:
        copy.wait()


here = (None, 0, 0)


def copied(matrices, places, shapes):
    moved = sum(2 * rows * columns for rows, columns in shapes)
    anywhere = pl.BlockSpec(memory_space=pl.ANY)
    return pl.pallas_call(
        functools.partial(copy_kernel, places),
        out_shape=[jax.ShapeDtypeStruct(shape, bf16) for shape in shapes],
        in_specs=[anywhere] * len(matrices),
        out_specs=[pl.BlockSpec(memory_space=pltpu.VMEM)] * len(shapes),
        scratch_shapes=[pltpu.SemaphoreType.DMA((len(shapes),))],
        cost_estimate=pl.CostEstimate(flops=0, bytes_accessed=2 * moved, transcendentals=0),
        compiler_params=pltpu.CompilerParams(vmem_limit_bytes=32 * 1024 * 1024),
        name="copied",
    )(*matrices)


def settled(value):
    return lax.optimization_barrier(value)


def fenced_all(values, after):
    return lax.optimization_barrier((*values, *after))[: len(values)]


def handed(value, steps):
    sections, count = lax.axis_size("section"), lax.axis_size("tensor")
    pairs = [
        (s * count + t, (s + 1) % sections * count + (t + steps) % count)
        for s in range(sections)
        for t in range(count)
    ]
    return lax.ppermute(value, ("section", "tensor"), pairs)


class Lane:
    def __init__(self, depth):
        self.depth = depth
        self.past = []

    def send(self, value, steps, after=(), depth=None, move=rotated):
        depth = depth or self.depth
        if len(self.past) >= depth:
            after = (self.past[-depth], *after)
        value = fenced(value, after)
        arrived = move(value, steps)
        self.past.append(arrived)
        return arrived


def dot(left, right):
    return jnp.dot(left, right, preferred_element_type=f32)


def dot_t(left, right):
    return lax.dot_general(left, right, (((1,), (1,)), ((), ())), preferred_element_type=f32)


def rows_at(matrix, start, size):
    return lax.dynamic_slice_in_dim(matrix, start, size, 0)


def cols_at(matrix, start, size):
    return lax.dynamic_slice_in_dim(matrix, start, size, 1)


def total(terms):
    result = terms[0]
    for term in terms[1:]:
        result = result + term
    return result


def soft_min(first, second):
    return 0.5 * (
        first + second - jnp.sqrt((first - second) * (first - second) + softness * softness)
    )


def soft_max(first, second):
    return 0.5 * (
        first + second + jnp.sqrt((first - second) * (first - second) + softness * softness)
    )


def soft_relu(difference):
    return 0.5 * (difference + jnp.sqrt(difference * difference + softness * softness))


def box_loss(logits, target):
    centre_x, centre_y, box_width, box_height = [jax.nn.sigmoid(v) * 1000.0 for v in logits]
    left, lower, right, upper = target
    left_pred = centre_x - 0.5 * box_width
    right_pred = centre_x + 0.5 * box_width
    lower_pred = centre_y - 0.5 * box_height
    upper_pred = centre_y + 0.5 * box_height
    inner_width = soft_relu(soft_min(right_pred, right) - soft_max(left_pred, left))
    inner_height = soft_relu(soft_min(upper_pred, upper) - soft_max(lower_pred, lower))
    intersection_area = inner_width * inner_height
    target_area = (right - left) * (upper - lower)
    union_area = box_width * box_height + target_area - intersection_area
    outer_width = soft_max(right_pred, right) - soft_min(left_pred, left)
    outer_height = soft_max(upper_pred, upper) - soft_min(lower_pred, lower)
    enclosing = outer_width * outer_height
    return 1.0 - intersection_area / union_area + (enclosing - union_area) / enclosing


def column(row):
    return jnp.transpose(jnp.broadcast_to(row, (128, row.shape[1])))[:, :1]


def gate_kernel(count, pairs, mine_ref, act_grad_ref, *refs):
    got_refs, refs = refs[: count - 1], refs[count - 1 :]
    left_refs, right_refs, refs = refs[:pairs], refs[pairs : 2 * pairs], refs[2 * pairs :]
    groups = mine_ref.shape[0] // act_grad_ref.shape[0]
    inverse_refs, (grad_ref, along_ref, *out_refs) = refs[:groups], refs[groups:]
    tokens = act_grad_ref.shape[0]
    pre = total([mine_ref[...]] + [ref[...].astype(f32) for ref in got_refs])
    first = pre[:tokens] * column(inverse_refs[0][...])
    gate = jax.nn.sigmoid(first)
    act_grad = total(
        [act_grad_ref[...]] + [dot_t(x[...], w[...]) for x, w in zip(left_refs, right_refs)]
    )
    grad = (act_grad * gate * (1.0 + first * (1.0 - gate))).astype(bf16)
    grad_ref[...] = grad
    along_ref[...] = lax.dot_general(
        jnp.ones((1, first.shape[1]), f32),
        grad.astype(f32) * first,
        (((1,), (1,)), ((), ())),
        precision=lax.Precision.HIGHEST,
        preferred_element_type=f32,
    )
    if groups > 1:
        second = pre[tokens:] * column(inverse_refs[1][...])
        out_refs[0][...] = (second * jax.nn.sigmoid(second)).astype(bf16)


def gated(mine, got, inverses, act_grad, left=(), right=()):
    tokens, hidden_width = act_grad.shape
    shapes = [
        jax.ShapeDtypeStruct((tokens, hidden_width), bf16),
        jax.ShapeDtypeStruct((1, tokens), f32),
    ]
    if mine.shape[0] > tokens:
        shapes.append(jax.ShapeDtypeStruct((mine.shape[0] - tokens, hidden_width), bf16))
    whole = pl.BlockSpec(memory_space=pltpu.VMEM)
    return pl.pallas_call(
        functools.partial(gate_kernel, len(got) + 1, len(left)),
        out_shape=shapes,
        in_specs=[whole] * (len(got) + 2 + 2 * len(left) + len(inverses)),
        out_specs=[whole] * len(shapes),
        compiler_params=pltpu.CompilerParams(vmem_limit_bytes=32 * 1024 * 1024),
        name="gated",
    )(mine, act_grad, *got, *left, *right, *inverses)


def head_kernel(count, full_width, *refs):
    pooled_refs, weight_refs = refs[:count], refs[count : 2 * count]
    gain_ref, bias_ref, target_ref, prompt_ref, keep_ref = refs[2 * count : 2 * count + 5]
    out_refs = refs[2 * count + 5 :]
    me = lax.axis_index("tensor")
    rows, width = pooled_refs[0].shape
    gains = []
    for k in range(count):
        start = pl.multiple_of(lax.rem(me + count - k, count) * width, width)
        gains.append(gain_ref[:, pl.ds(start, width)])
    for row in range(rows):
        weights = pool_weights(prompt_ref[row], keep_ref[row : row + 1, :])
        inverse_count = 1.0 / jnp.sum(weights, axis=1, keepdims=True)
        pooled = [ref[row : row + 1, :] * inverse_count for ref in pooled_refs]
        square = total([jnp.sum(p * p, axis=1, keepdims=True) for p in pooled])
        inverse = lax.rsqrt(square / full_width + epsilon)
        projected = inverse * total(
            [
                jnp.sum((p * g) * w[...], axis=1, keepdims=True)
                for p, g, w in zip(pooled, gains, weight_refs)
            ]
        )
        projected = [projected[j : j + 1, :] for j in range(4)]
        target = [target_ref[row, j].astype(f32) for j in range(4)]
        logits = [projected[j] + bias_ref[j] for j in range(4)]
        _, pullback = jax.vjp(lambda *values: box_loss(values, target), *logits)
        logit_grad = pullback(jnp.full((1, 1), loss_scale / rows, f32))
        row_mean = total([logit_grad[j] * projected[j] for j in range(4)]) / full_width
        for p, g, w, out in zip(pooled, gains, weight_refs, out_refs):
            scaled_grad = total([logit_grad[j] * w[j : j + 1, :] for j in range(4)])
            out[row : row + 1, :] = (
                inverse * (g * scaled_grad - p * inverse * row_mean) * inverse_count
            )


def pool_weights(prompt_length, keep_row):
    positions = lax.broadcasted_iota(jnp.int32, keep_row.shape, 1)
    starting = jnp.where(positions == prompt_length - 1, 1.0, 0.0)
    kept = jnp.where(positions >= prompt_length, 1.0, 0.0)
    return starting + kept * keep_row.astype(f32)


def head_rows(pooled, weights, head_gain, head_bias, target_box, prompt_length, keep_mask, full_width):
    count = len(pooled)
    whole = pl.BlockSpec(memory_space=pltpu.VMEM)
    scalars = pl.BlockSpec(memory_space=pltpu.SMEM)
    rows = pl.pallas_call(
        functools.partial(head_kernel, count, full_width),
        out_shape=[jax.ShapeDtypeStruct(p.shape, f32) for p in pooled],
        in_specs=[whole] * (2 * count + 1) + [scalars] * 3 + [whole],
        out_specs=[whole] * count,
        name="head",
    )(*pooled, *weights, head_gain[None, :], head_bias, target_box, prompt_length, keep_mask)
    return [row.astype(bf16) for row in rows]


def per_device(
    forward_input,
    saved_last,
    saved_first,
    first_cotangent,
    section_entry,
    last_gain,
    last_up,
    last_down,
    first_gain,
    first_up,
    first_down,
    head_gain,
    head_weight,
    head_bias,
    prompt_length,
    keep_mask,
    target_box,
):
    count = lax.axis_size("tensor")
    me = lax.axis_index("tensor")
    section_index = lax.axis_index("section")
    opening = section_index == 0
    closing = section_index == lax.axis_size("section") - 1
    entering, saved, cotangent = forward_input[0], saved_first[0], first_cotangent[0]
    last_up, last_down, first_up, first_down = last_up[0], last_down[0], first_up[0], first_down[0]
    tokens, width = entering.shape
    full_width = width * count
    hidden_width = last_up.shape[1]
    chunk = min(width, chunk_width)
    pieces = range(width // chunk)
    final = pieces[-1]
    others = range(1, count)
    after = [lax.rem(me + k, count) for k in range(count)]
    before = [lax.rem(me + count - k, count) for k in range(count)]

    def piece(values, j):
        return values[:, j * chunk : (j + 1) * chunk]

    def square_sum(values):
        values = values.astype(f32)
        return jnp.sum(values * values, axis=1)

    lane = Lane(2)
    first_gain_cols = rows_at(first_gain[0], me * width, width)
    last_gain_cols = rows_at(last_gain[0], me * width, width)

    def scaled(values, gain_cols):
        return (values.astype(f32) * gain_cols).astype(bf16)

    def gain_piece(gain_cols, j):
        return gain_cols[j * chunk : (j + 1) * chunk]

    def up_parts(up_matrix, sizes):
        starts = [sum(sizes[:cut]) for cut in range(len(sizes))]
        places = [(0, (k, width, start), here) for start in starts for k in others]
        shapes = [(size, hidden_width) for size in sizes for k in others]
        places.append((0, (0, width, 0), here))
        shapes.append((width, hidden_width))
        parts = copied([up_matrix], places, shapes)
        step = count - 1
        return [parts[i * step : (i + 1) * step] for i in range(len(sizes))], parts[-1]

    def down_parts(down_matrix):
        places = [(0, here, (k, width, 0)) for k in range(count)]
        return copied([down_matrix], places, [(hidden_width, width)] * count)

    def send_up(parts, ahead=(), depth=None):
        return [lane.send(part, k, ahead, depth) for part, k in zip(parts, others)]

    def up_rows(own, got, start, size):
        blocks = [own[start : start + size]]
        for cuts in zip(*got):
            taken, at = [], 0
            for cut in cuts:
                low, high = max(start - at, 0), min(start + size - at, cut.shape[0])
                if low < high:
                    taken.append(cut[low:high])
                at += cut.shape[0]
            blocks.append(taken[0] if len(taken) == 1 else jnp.concatenate(taken, axis=0))
        return blocks

    def exchange_cols(values, ahead=()):
        return [values] + [lane.send(values, k, ahead) for k in others]

    def sum_small(values):
        return total([values] + [rotated(values, k) for k in others])

    def collect(sent):
        return [lane.send(t, -k) for t, k in zip(sent, others)]

    def exchange_grad(pre_grad, along):
        blocks = [pre_grad] + [lane.send(pre_grad, k) for k in others]
        return blocks, sum_small(along)[0] / full_width

    def other_products(normed, got, after=()):
        sums = []
        for cuts in zip(*got):
            terms, at = [], 0
            for cut in cuts[:-1]:
                terms.append(dot(normed[:, at : at + cut.shape[0]], cut))
                at += cut.shape[0]
            early = [settled(total(terms))] if terms else []
            last = dot(fenced(normed[:, at:], [*early, *after]), cuts[-1])
            sums.append(total([*early, last]).astype(bf16))
        return sums

    def input_grad(values, given, inverse, gain_cols, blocks, along, up_blocks):
        norm_grad = total([dot_t(blocks[k], up_blocks[k]) for k in range(count)])
        unit = values.astype(f32) * inverse[:, None]
        return (
            given.astype(f32)
            + inverse[:, None] * (gain_cols * norm_grad - unit * along[:, None])
        ).astype(bf16)

    def send_out(activated, downs, j):
        values = [dot(activated, piece(downs[k], j)).astype(bf16) for k in others]
        depth = 3 if j < 2 else 2
        return [lane.send(value, k, depth=depth, move=handed) for value, k in zip(values, others)]

    def add_out(values, mine, terms):
        return (values.astype(f32) + total([mine] + [t.astype(f32) for t in terms])).astype(bf16)

    def act_grad_terms(blocks, downs):
        return [dot_t(blocks[k], downs[-k]) for k in range(count)]

    stored = jnp.where(closing, entering, saved_last[0])

    last_parts, last_up_own = up_parts(last_up, [width // 2] * 2)
    cotangents = exchange_cols(cotangent)
    last_got = [send_up(last_parts[0])]
    last_downs = down_parts(last_down)
    first_parts, first_up_own = up_parts(first_up, [width // 4, width // 4, width // 2])
    first_downs = down_parts(first_down)
    squares = jnp.stack([square_sum(saved), square_sum(entering), square_sum(stored)])
    head_weights = [head_weight.T]
    entering_scaled = scaled(entering, last_gain_cols)
    stored_scaled = scaled(stored, last_gain_cols)
    first_saved = scaled(saved, first_gain_cols)

    last_got.append(send_up(last_parts[1]))
    ahead = [
        *last_downs, first_up_own, *first_downs, squares, *head_weights, entering_scaled,
        stored_scaled, first_saved,
    ]
    first_got = [send_up(first_parts[0], ahead)]
    sent = other_products(entering_scaled, last_got)
    mine = dot(fenced(entering_scaled, sent), last_up_own)
    got = collect(sent)
    squares = fenced(squares, sent)
    squares = total([squares] + [rotated(squares, k) for k in others])
    inverses = lax.rsqrt(squares / full_width + epsilon)
    head_weights += [rotated(fenced(head_weights[0], sent), k) for k in others]
    act_grad = total(act_grad_terms(cotangents, first_downs))
    first_got.append(send_up(first_parts[1], sent))
    stored_sent = other_products(fenced(stored_scaled, sent), last_got)
    stored_mine = dot(fenced(stored_scaled, sent), last_up_own)
    stored_got = collect(stored_sent)
    inverse_rows = [settled(inverses[i : i + 1]) for i in range(3)]
    first_gains = [settled(gain_piece(first_gain_cols, j)) for j in pieces]
    last_up_got = [settled(jnp.concatenate(cuts, axis=0)) for cuts in zip(*last_got)]
    right = [settled(piece(last_downs[-k], final)) for k in others]
    got = fenced_all(got, [*right, *last_up_got, *stored_sent, stored_mine, act_grad, *inverse_rows, *first_gains, last_gain_cols, *head_weights[1:]])
    entering_pre = total([mine] + [t.astype(f32) for t in got]) * inverses[1][:, None]

    activated = jax.nn.silu(entering_pre).astype(bf16)
    mine = handed((entering.astype(f32) + dot(activated, last_downs[0])).astype(bf16), 0)
    gots = [send_out(activated, last_downs, j) for j in pieces]
    first_got.append(send_up(first_parts[2], depth=3))
    incoming = [jnp.concatenate(t, axis=1).astype(f32) for t in zip(*gots)]
    incoming = total([mine.astype(f32)] + incoming).astype(bf16)
    entry = jnp.where(opening, section_entry, incoming)

    row_count, row_length = keep_mask.shape
    token_weights = jnp.concatenate(
        [pool_weights(prompt_length[row], keep_mask[row : row + 1]) for row in range(row_count)], 0
    )

    def pool(values):
        weights = token_weights.astype(bf16)
        if row_count == 1:
            return dot(weights, values)
        values = values.reshape(row_count, row_length, values.shape[1])
        return jnp.einsum("rt,rtd->rd", weights, values, preferred_element_type=f32)

    def on_tokens(rows):
        values = token_weights[:, :, None] * rows.astype(f32)[:, None, :]
        return values.reshape(tokens, rows.shape[1])

    back = lax.axis_size("section") - 1
    pooled = lax.ppermute(pool(fenced(incoming, [entry])), "section", [(0, back)])

    entry_squares = sum_small(square_sum(entry)[None, :])
    entry_inverse = settled(lax.rsqrt(entry_squares / full_width + epsilon))
    pair = jnp.concatenate([first_saved, scaled(entry, first_gain_cols)], axis=0)
    sent = other_products(pair, first_got, [entry_inverse])
    mine = dot(fenced(pair, sent), first_up_own)
    got = collect(sent)
    pooled = fenced(pooled, sent)
    pooled = [pooled] + [rotated(pooled, k) for k in others]

    pre_grad, along, entry_activated = gated(mine, got, [inverse_rows[0], entry_inverse], act_grad)
    first_blocks, first_along = exchange_grad(pre_grad, along)
    early = (len(pieces) + 1) // 2

    def first_out(low, high, activated):
        columns = slice(low * chunk, high * chunk)
        values = [dot(activated, first_downs[k][:, columns]).astype(bf16) for k in others]
        return [lane.send(value, k) for value, k in zip(values, others)]

    gots = [first_out(0, early, entry_activated)]
    returned = []
    for j in pieces:
        gradient = input_grad(
            piece(saved, j),
            piece(cotangent, j),
            inverses[0],
            first_gains[j],
            fenced_all(first_blocks, returned[-1:]),
            first_along,
            up_rows(first_up_own, first_got, j * chunk, chunk),
        )
        returned.append(gradient)
    returned = [shifted(gradient, "section", -1) for gradient in returned]

    act_grads = []
    for j in pieces[:-1]:
        ahead = act_grads[j - 2 : j - 1] if j > 1 else ()
        blocks = exchange_cols(returned[j], ahead)
        terms = act_grad_terms(blocks, [piece(d, j) for d in last_downs])
        act_grads.append(total(act_grads[-1:] + terms))
        if j == 0:
            late = blocks[1:]
    if final == 0:
        late = first_blocks[1:]
    head_grads = head_rows(
        fenced_all(pooled, late),
        head_weights,
        head_gain,
        head_bias,
        target_box,
        prompt_length,
        keep_mask,
        full_width,
    )
    head_act_grad = total([dot_t(head_grads[k], last_downs[-k]) for k in range(count)])
    given = settled(
        jnp.where(
            closing, on_tokens(head_grads[0]).astype(bf16), jnp.concatenate(returned, axis=1)
        )
    )
    act_grad = settled(
        total(
            [
                jnp.where(closing, on_tokens(head_act_grad), 0.0),
                dot_t(returned[-1], piece(last_downs[0], final)),
                *act_grads[-1:],
            ]
        )
    )
    activated_late = fenced(entry_activated, late)
    if early < final:
        gots.append(first_out(early, final, activated_late))
    ahead = [given, act_grad, *right, *(gots[-1] if early < final else ())]
    left = exchange_cols(returned[-1], ahead)[1:]
    pre_grad, along = gated(stored_mine, stored_got, inverse_rows[2:], act_grad, left, right)
    last_blocks, last_along = exchange_grad(pre_grad, along)
    if early <= final:
        gots.append(first_out(max(early, final), len(pieces), activated_late))
    outs, at = [], 0
    for got in gots[:-1]:
        columns = slice(at, at + got[0].shape[1])
        mine = dot(activated_late, first_downs[0][:, columns])
        outs.append(add_out(entry[:, columns], mine, got))
        at = columns.stop
    mine = settled(dot(activated_late, first_downs[0][:, at:]))
    outs = jnp.concatenate([*outs, entry[:, at:]], axis=1)
    got = fenced_all(gots[-1], [mine, outs])
    layer_output = lax.dynamic_update_slice_in_dim(outs, add_out(entry[:, at:], mine, got), at, 1)

    own = settled(dot_t(last_blocks[0], last_up_own))
    norm_grad = total(
        [own] + [dot_t(block, got) for block, got in zip(last_blocks[1:], last_up_got)]
    )
    unit = stored.astype(f32) * inverses[2][:, None]
    input_gradient = (
        given.astype(f32)
        + inverses[2][:, None] * (last_gain_cols * norm_grad - unit * last_along[:, None])
    ).astype(bf16)
    return (layer_output[None], input_gradient[None])


def solution(mesh):
    placed = (
        P("section", None, "tensor"),
        P("section", None, "tensor"),
        P("section", None, "tensor"),
        P("section", None, "tensor"),
        P(None, "tensor"),
        P("section", None),
        P("section", None, "tensor"),
        P("section", "tensor", None),
        P("section", None),
        P("section", None, "tensor"),
        P("section", "tensor", None),
        P(),
        P("tensor", None),
        P(),
        P(),
        P(),
        P(),
    )
    return jax.shard_map(
        per_device,
        mesh=mesh,
        in_specs=placed,
        out_specs=(P("section", None, "tensor"), P("section", None, "tensor")),
        check_vma=False,
    )
```

```python
import functools

import jax
import jax.numpy as jnp
from jax import lax
from jax.experimental import pallas as pl
from jax.experimental.pallas import tpu as pltpu
from jax.sharding import PartitionSpec as P

epsilon = 1e-06
softness = 4.0
loss_scale = 4096.0
chunk_width = 1024

f32 = jnp.float32
bf16 = jnp.bfloat16


def shifted(value, axis, steps):
    count = lax.axis_size(axis)
    initial, last = (max(0, -steps), min(count, count - steps))
    return lax.ppermute(value, axis, [(source, source + steps) for source in range(initial, last)])


def rotated(value, steps):
    count = lax.axis_size("tensor")
    return lax.ppermute(value, "tensor", [(i, (i + steps) % count) for i in range(count)])


def fenced(value, after):
    return lax.optimization_barrier((value, *after))[0] if after else value


def copy_kernel(places, *refs):
    sources, targets, sems = refs[: -len(places) - 1], refs[-len(places) - 1 : -1], refs[-1]
    count, me = lax.axis_size("tensor"), lax.axis_index("tensor")
    copies = []
    for slot, (number, row, column) in enumerate(places):
        rows, columns = targets[slot].shape
        starts = []
        for size, (away, width, offset) in zip((rows, columns), (row, column)):
            start = offset if away is None else lax.rem(me + away, count) * width + offset
            starts.append(pl.ds(start if away is None else pl.multiple_of(start, 128), size))
        source = sources[number].at[starts[0], starts[1]]
        copies.append(pltpu.make_async_copy(source, targets[slot], sems.at[slot]))
    for copy in copies:
        copy.start()
    for copy in copies:
        copy.wait()


here = (None, 0, 0)


def copied(matrices, places, shapes):
    moved = sum(2 * rows * columns for rows, columns in shapes)
    anywhere = pl.BlockSpec(memory_space=pl.ANY)
    return pl.pallas_call(
        functools.partial(copy_kernel, places),
        out_shape=[jax.ShapeDtypeStruct(shape, bf16) for shape in shapes],
        in_specs=[anywhere] * len(matrices),
        out_specs=[pl.BlockSpec(memory_space=pltpu.VMEM)] * len(shapes),
        scratch_shapes=[pltpu.SemaphoreType.DMA((len(shapes),))],
        cost_estimate=pl.CostEstimate(flops=0, bytes_accessed=2 * moved, transcendentals=0),
        compiler_params=pltpu.CompilerParams(vmem_limit_bytes=32 * 1024 * 1024),
        name="copied",
    )(*matrices)


def settled(value):
    return lax.optimization_barrier(value)


def fenced_all(values, after):
    return lax.optimization_barrier((*values, *after))[: len(values)]


class Lane:
    def __init__(self, depth):
        self.depth = depth
        self.past = []

    def send(self, value, steps, after=(), depth=None):
        depth = depth or self.depth
        if len(self.past) >= depth:
            after = (self.past[-depth], *after)
        value = fenced(value, after)
        arrived = rotated(value, steps)
        self.past.append(arrived)
        return arrived


def dot(left, right):
    return jnp.dot(left, right, preferred_element_type=f32)


def dot_t(left, right):
    return lax.dot_general(left, right, (((1,), (1,)), ((), ())), preferred_element_type=f32)


def rows_at(matrix, start, size):
    return lax.dynamic_slice_in_dim(matrix, start, size, 0)


def cols_at(matrix, start, size):
    return lax.dynamic_slice_in_dim(matrix, start, size, 1)


def total(terms):
    result = terms[0]
    for term in terms[1:]:
        result = result + term
    return result


def soft_min(first, second):
    return 0.5 * (
        first + second - jnp.sqrt((first - second) * (first - second) + softness * softness)
    )


def soft_max(first, second):
    return 0.5 * (
        first + second + jnp.sqrt((first - second) * (first - second) + softness * softness)
    )


def soft_relu(difference):
    return 0.5 * (difference + jnp.sqrt(difference * difference + softness * softness))


def box_loss(logits, target):
    centre_x, centre_y, box_width, box_height = [jax.nn.sigmoid(v) * 1000.0 for v in logits]
    left, lower, right, upper = target
    left_pred = centre_x - 0.5 * box_width
    right_pred = centre_x + 0.5 * box_width
    lower_pred = centre_y - 0.5 * box_height
    upper_pred = centre_y + 0.5 * box_height
    inner_width = soft_relu(soft_min(right_pred, right) - soft_max(left_pred, left))
    inner_height = soft_relu(soft_min(upper_pred, upper) - soft_max(lower_pred, lower))
    intersection_area = inner_width * inner_height
    target_area = (right - left) * (upper - lower)
    union_area = box_width * box_height + target_area - intersection_area
    outer_width = soft_max(right_pred, right) - soft_min(left_pred, left)
    outer_height = soft_max(upper_pred, upper) - soft_min(lower_pred, lower)
    enclosing = outer_width * outer_height
    return 1.0 - intersection_area / union_area + (enclosing - union_area) / enclosing


def column(row):
    return jnp.transpose(jnp.broadcast_to(row, (128, row.shape[1])))[:, :1]


def gate_kernel(count, pairs, mine_ref, act_grad_ref, *refs):
    got_refs, refs = refs[: count - 1], refs[count - 1 :]
    left_refs, right_refs, refs = refs[:pairs], refs[pairs : 2 * pairs], refs[2 * pairs :]
    groups = mine_ref.shape[0] // act_grad_ref.shape[0]
    inverse_refs, (grad_ref, along_ref, *out_refs) = refs[:groups], refs[groups:]
    tokens = act_grad_ref.shape[0]
    pre = total([mine_ref[...]] + [ref[...].astype(f32) for ref in got_refs])
    first = pre[:tokens] * column(inverse_refs[0][...])
    gate = jax.nn.sigmoid(first)
    act_grad = total(
        [act_grad_ref[...]] + [dot_t(x[...], w[...]) for x, w in zip(left_refs, right_refs)]
    )
    grad = (act_grad * gate * (1.0 + first * (1.0 - gate))).astype(bf16)
    grad_ref[...] = grad
    along_ref[...] = lax.dot_general(
        jnp.ones((1, first.shape[1]), f32),
        grad.astype(f32) * first,
        (((1,), (1,)), ((), ())),
        precision=lax.Precision.HIGHEST,
        preferred_element_type=f32,
    )
    if groups > 1:
        second = pre[tokens:] * column(inverse_refs[1][...])
        out_refs[0][...] = (second * jax.nn.sigmoid(second)).astype(bf16)


def gated(mine, got, inverses, act_grad, left=(), right=()):
    tokens, hidden_width = act_grad.shape
    shapes = [
        jax.ShapeDtypeStruct((tokens, hidden_width), bf16),
        jax.ShapeDtypeStruct((1, tokens), f32),
    ]
    if mine.shape[0] > tokens:
        shapes.append(jax.ShapeDtypeStruct((mine.shape[0] - tokens, hidden_width), bf16))
    whole = pl.BlockSpec(memory_space=pltpu.VMEM)
    return pl.pallas_call(
        functools.partial(gate_kernel, len(got) + 1, len(left)),
        out_shape=shapes,
        in_specs=[whole] * (len(got) + 2 + 2 * len(left) + len(inverses)),
        out_specs=[whole] * len(shapes),
        compiler_params=pltpu.CompilerParams(vmem_limit_bytes=32 * 1024 * 1024),
        name="gated",
    )(mine, act_grad, *got, *left, *right, *inverses)


def head_kernel(count, full_width, *refs):
    pooled_refs, weight_refs = refs[:count], refs[count : 2 * count]
    gain_ref, bias_ref, target_ref, prompt_ref, keep_ref = refs[2 * count : 2 * count + 5]
    out_refs = refs[2 * count + 5 :]
    me = lax.axis_index("tensor")
    rows, width = pooled_refs[0].shape
    gains = []
    for k in range(count):
        start = pl.multiple_of(lax.rem(me + count - k, count) * width, width)
        gains.append(gain_ref[:, pl.ds(start, width)])
    for row in range(rows):
        weights = pool_weights(prompt_ref[row], keep_ref[row : row + 1, :])
        inverse_count = 1.0 / jnp.sum(weights, axis=1, keepdims=True)
        pooled = [ref[row : row + 1, :] * inverse_count for ref in pooled_refs]
        square = total([jnp.sum(p * p, axis=1, keepdims=True) for p in pooled])
        inverse = lax.rsqrt(square / full_width + epsilon)
        projected = inverse * total(
            [
                jnp.sum((p * g) * w[...], axis=1, keepdims=True)
                for p, g, w in zip(pooled, gains, weight_refs)
            ]
        )
        projected = [projected[j : j + 1, :] for j in range(4)]
        target = [target_ref[row, j].astype(f32) for j in range(4)]
        logits = [projected[j] + bias_ref[j] for j in range(4)]
        _, pullback = jax.vjp(lambda *values: box_loss(values, target), *logits)
        logit_grad = pullback(jnp.full((1, 1), loss_scale / rows, f32))
        row_mean = total([logit_grad[j] * projected[j] for j in range(4)]) / full_width
        for p, g, w, out in zip(pooled, gains, weight_refs, out_refs):
            scaled_grad = total([logit_grad[j] * w[j : j + 1, :] for j in range(4)])
            out[row : row + 1, :] = (
                inverse * (g * scaled_grad - p * inverse * row_mean) * inverse_count
            )


def pool_weights(prompt_length, keep_row):
    positions = lax.broadcasted_iota(jnp.int32, keep_row.shape, 1)
    starting = jnp.where(positions == prompt_length - 1, 1.0, 0.0)
    kept = jnp.where(positions >= prompt_length, 1.0, 0.0)
    return starting + kept * keep_row.astype(f32)


def head_rows(pooled, weights, head_gain, head_bias, target_box, prompt_length, keep_mask, full_width):
    count = len(pooled)
    whole = pl.BlockSpec(memory_space=pltpu.VMEM)
    scalars = pl.BlockSpec(memory_space=pltpu.SMEM)
    rows = pl.pallas_call(
        functools.partial(head_kernel, count, full_width),
        out_shape=[jax.ShapeDtypeStruct(p.shape, f32) for p in pooled],
        in_specs=[whole] * (2 * count + 1) + [scalars] * 3 + [whole],
        out_specs=[whole] * count,
        name="head",
    )(*pooled, *weights, head_gain[None, :], head_bias, target_box, prompt_length, keep_mask)
    return [row.astype(bf16) for row in rows]


def per_device(
    forward_input,
    saved_last,
    saved_first,
    first_cotangent,
    section_entry,
    last_gain,
    last_up,
    last_down,
    first_gain,
    first_up,
    first_down,
    head_gain,
    head_weight,
    head_bias,
    prompt_length,
    keep_mask,
    target_box,
):
    count = lax.axis_size("tensor")
    me = lax.axis_index("tensor")
    section_index = lax.axis_index("section")
    opening = section_index == 0
    closing = section_index == lax.axis_size("section") - 1
    entering, saved, cotangent = forward_input[0], saved_first[0], first_cotangent[0]
    last_up, last_down, first_up, first_down = last_up[0], last_down[0], first_up[0], first_down[0]
    tokens, width = entering.shape
    full_width = width * count
    hidden_width = last_up.shape[1]
    chunk = min(width, chunk_width)
    pieces = range(width // chunk)
    final = pieces[-1]
    others = range(1, count)
    after = [lax.rem(me + k, count) for k in range(count)]
    before = [lax.rem(me + count - k, count) for k in range(count)]

    def piece(values, j):
        return values[:, j * chunk : (j + 1) * chunk]

    def square_sum(values):
        values = values.astype(f32)
        return jnp.sum(values * values, axis=1)

    lane = Lane(2)
    first_gain_cols = rows_at(first_gain[0], me * width, width)
    last_gain_cols = rows_at(last_gain[0], me * width, width)

    def scaled(values, gain_cols):
        return (values.astype(f32) * gain_cols).astype(bf16)

    def gain_piece(gain_cols, j):
        return gain_cols[j * chunk : (j + 1) * chunk]

    def up_parts(up_matrix, sizes):
        starts = [sum(sizes[:cut]) for cut in range(len(sizes))]
        places = [(0, (k, width, start), here) for start in starts for k in others]
        shapes = [(size, hidden_width) for size in sizes for k in others]
        places.append((0, (0, width, 0), here))
        shapes.append((width, hidden_width))
        parts = copied([up_matrix], places, shapes)
        step = count - 1
        return [parts[i * step : (i + 1) * step] for i in range(len(sizes))], parts[-1]

    def down_parts(down_matrix):
        places = [(0, here, (k, width, 0)) for k in range(count)]
        return copied([down_matrix], places, [(hidden_width, width)] * count)

    def send_up(parts, ahead=(), depth=None):
        return [lane.send(part, k, ahead, depth) for part, k in zip(parts, others)]

    def up_rows(own, got, start, size):
        blocks = [own[start : start + size]]
        for cuts in zip(*got):
            taken, at = [], 0
            for cut in cuts:
                low, high = max(start - at, 0), min(start + size - at, cut.shape[0])
                if low < high:
                    taken.append(cut[low:high])
                at += cut.shape[0]
            blocks.append(taken[0] if len(taken) == 1 else jnp.concatenate(taken, axis=0))
        return blocks

    def exchange_cols(values, ahead=()):
        return [values] + [lane.send(values, k, ahead) for k in others]

    def sum_small(values):
        return total([values] + [rotated(values, k) for k in others])

    def collect(sent):
        return [lane.send(t, -k) for t, k in zip(sent, others)]

    def exchange_grad(pre_grad, along):
        blocks = [pre_grad] + [lane.send(pre_grad, k) for k in others]
        return blocks, sum_small(along)[0] / full_width

    def other_products(normed, got, after=()):
        sums = []
        for cuts in zip(*got):
            terms, at = [], 0
            for cut in cuts[:-1]:
                terms.append(dot(normed[:, at : at + cut.shape[0]], cut))
                at += cut.shape[0]
            early = [settled(total(terms))] if terms else []
            last = dot(fenced(normed[:, at:], [*early, *after]), cuts[-1])
            sums.append(total([*early, last]).astype(bf16))
        return sums

    def input_grad(values, given, inverse, gain_cols, blocks, along, up_blocks):
        norm_grad = total([dot_t(blocks[k], up_blocks[k]) for k in range(count)])
        unit = values.astype(f32) * inverse[:, None]
        return (
            given.astype(f32)
            + inverse[:, None] * (gain_cols * norm_grad - unit * along[:, None])
        ).astype(bf16)

    def send_out(activated, downs, j, ahead=()):
        values = [dot(activated, piece(downs[k], j)).astype(bf16) for k in others]
        depth = 3 if j < 2 else 2
        return [lane.send(value, k, ahead, depth) for value, k in zip(values, others)]

    def add_out(values, mine, terms):
        return (values.astype(f32) + total([mine] + [t.astype(f32) for t in terms])).astype(bf16)

    def act_grad_terms(blocks, downs):
        return [dot_t(blocks[k], downs[-k]) for k in range(count)]

    stored = jnp.where(closing, entering, saved_last[0])

    last_parts, last_up_own = up_parts(last_up, [width // 2] * 2)
    cotangents = exchange_cols(cotangent)
    last_got = [send_up(last_parts[0])]
    last_downs = down_parts(last_down)
    first_parts, first_up_own = up_parts(first_up, [width // 4, width // 4, width // 2])
    first_downs = down_parts(first_down)
    squares = jnp.stack([square_sum(saved), square_sum(entering), square_sum(stored)])
    head_weights = [head_weight.T]
    entering_scaled = scaled(entering, last_gain_cols)
    stored_scaled = scaled(stored, last_gain_cols)
    first_saved = scaled(saved, first_gain_cols)

    last_got.append(send_up(last_parts[1]))
    ahead = [
        *last_downs, first_up_own, *first_downs, squares, *head_weights, entering_scaled,
        stored_scaled, first_saved,
    ]
    first_got = [send_up(first_parts[0], ahead)]
    sent = other_products(entering_scaled, last_got)
    mine = dot(fenced(entering_scaled, sent), last_up_own)
    got = collect(sent)
    squares = fenced(squares, sent)
    squares = total([squares] + [rotated(squares, k) for k in others])
    inverses = lax.rsqrt(squares / full_width + epsilon)
    head_weights += [rotated(fenced(head_weights[0], sent), k) for k in others]
    act_grad = total(act_grad_terms(cotangents, first_downs))
    first_got.append(send_up(first_parts[1], sent))
    stored_sent = other_products(fenced(stored_scaled, sent), last_got)
    stored_mine = dot(fenced(stored_scaled, sent), last_up_own)
    stored_got = collect(stored_sent)
    inverse_rows = [settled(inverses[i : i + 1]) for i in range(3)]
    first_gains = [settled(gain_piece(first_gain_cols, j)) for j in pieces]
    last_up_got = [settled(jnp.concatenate(cuts, axis=0)) for cuts in zip(*last_got)]
    right = [settled(piece(last_downs[-k], final)) for k in others]
    got = fenced_all(got, [*right, *last_up_got, *stored_sent, stored_mine, act_grad, *inverse_rows, *first_gains, last_gain_cols, *head_weights[1:]])
    entering_pre = total([mine] + [t.astype(f32) for t in got]) * inverses[1][:, None]

    activated = jax.nn.silu(entering_pre).astype(bf16)
    gots = [send_out(activated, last_downs, j) for j in pieces[:-1]]
    mine = dot(activated, last_downs[0])
    gots.append(send_out(activated, last_downs, final, [mine]))
    first_got.append(send_up(first_parts[2], depth=3))
    hidden = add_out(entering, mine, [jnp.concatenate(t, axis=1) for t in zip(*gots)])
    entry = jnp.where(opening, section_entry, shifted(hidden, "section", 1))

    row_count, row_length = keep_mask.shape
    token_weights = jnp.concatenate(
        [pool_weights(prompt_length[row], keep_mask[row : row + 1]) for row in range(row_count)], 0
    )

    def pool(values):
        weights = token_weights.astype(bf16)
        if row_count == 1:
            return dot(weights, values)
        values = values.reshape(row_count, row_length, values.shape[1])
        return jnp.einsum("rt,rtd->rd", weights, values, preferred_element_type=f32)

    def on_tokens(rows):
        values = token_weights[:, :, None] * rows.astype(f32)[:, None, :]
        return values.reshape(tokens, rows.shape[1])

    pooled = pool(fenced(hidden, [entry]))

    entry_squares = sum_small(square_sum(entry)[None, :])
    entry_inverse = settled(lax.rsqrt(entry_squares / full_width + epsilon))
    pair = jnp.concatenate([first_saved, scaled(entry, first_gain_cols)], axis=0)
    sent = other_products(pair, first_got, [entry_inverse])
    mine = dot(fenced(pair, sent), first_up_own)
    got = collect(sent)
    pooled = fenced(pooled, sent)
    pooled = [pooled] + [rotated(pooled, k) for k in others]

    pre_grad, along, entry_activated = gated(mine, got, [inverse_rows[0], entry_inverse], act_grad)
    first_blocks, first_along = exchange_grad(pre_grad, along)
    early = (len(pieces) + 1) // 2

    def first_out(low, high, activated):
        columns = slice(low * chunk, high * chunk)
        values = [dot(activated, first_downs[k][:, columns]).astype(bf16) for k in others]
        return [lane.send(value, k) for value, k in zip(values, others)]

    gots = [first_out(0, early, entry_activated)]
    returned = []
    for j in pieces:
        gradient = input_grad(
            piece(saved, j),
            piece(cotangent, j),
            inverses[0],
            first_gains[j],
            fenced_all(first_blocks, returned[-1:]),
            first_along,
            up_rows(first_up_own, first_got, j * chunk, chunk),
        )
        returned.append(gradient)
    returned = [shifted(gradient, "section", -1) for gradient in returned]

    act_grads = []
    for j in pieces[:-1]:
        ahead = act_grads[j - 2 : j - 1] if j > 1 else ()
        blocks = exchange_cols(returned[j], ahead)
        terms = act_grad_terms(blocks, [piece(d, j) for d in last_downs])
        act_grads.append(total(act_grads[-1:] + terms))
        if j == 0:
            late = blocks[1:]
    if final == 0:
        late = first_blocks[1:]
    head_grads = head_rows(
        fenced_all(pooled, late),
        head_weights,
        head_gain,
        head_bias,
        target_box,
        prompt_length,
        keep_mask,
        full_width,
    )
    head_act_grad = total([dot_t(head_grads[k], last_downs[-k]) for k in range(count)])
    given = settled(
        jnp.where(
            closing, on_tokens(head_grads[0]).astype(bf16), jnp.concatenate(returned, axis=1)
        )
    )
    act_grad = settled(
        total(
            [
                jnp.where(closing, on_tokens(head_act_grad), 0.0),
                dot_t(returned[-1], piece(last_downs[0], final)),
                *act_grads[-1:],
            ]
        )
    )
    activated_late = fenced(entry_activated, late)
    if early < final:
        gots.append(first_out(early, final, activated_late))
    ahead = [given, act_grad, *right, *(gots[-1] if early < final else ())]
    left = exchange_cols(returned[-1], ahead)[1:]
    pre_grad, along = gated(stored_mine, stored_got, inverse_rows[2:], act_grad, left, right)
    last_blocks, last_along = exchange_grad(pre_grad, along)
    if early <= final:
        gots.append(first_out(max(early, final), len(pieces), activated_late))
    outs, at = [], 0
    for got in gots[:-1]:
        columns = slice(at, at + got[0].shape[1])
        mine = dot(activated_late, first_downs[0][:, columns])
        outs.append(add_out(entry[:, columns], mine, got))
        at = columns.stop
    mine = settled(dot(activated_late, first_downs[0][:, at:]))
    outs = jnp.concatenate([*outs, entry[:, at:]], axis=1)
    got = fenced_all(gots[-1], [mine, outs])
    layer_output = lax.dynamic_update_slice_in_dim(outs, add_out(entry[:, at:], mine, got), at, 1)

    own = settled(dot_t(last_blocks[0], last_up_own))
    norm_grad = total(
        [own] + [dot_t(block, got) for block, got in zip(last_blocks[1:], last_up_got)]
    )
    unit = stored.astype(f32) * inverses[2][:, None]
    input_gradient = (
        given.astype(f32)
        + inverses[2][:, None] * (last_gain_cols * norm_grad - unit * last_along[:, None])
    ).astype(bf16)
    return (layer_output[None], input_gradient[None])


def solution(mesh):
    placed = (
        P("section", None, "tensor"),
        P("section", None, "tensor"),
        P("section", None, "tensor"),
        P("section", None, "tensor"),
        P(None, "tensor"),
        P("section", None),
        P("section", None, "tensor"),
        P("section", "tensor", None),
        P("section", None),
        P("section", None, "tensor"),
        P("section", "tensor", None),
        P(),
        P("tensor", None),
        P(),
        P(),
        P(),
        P(),
    )
    return jax.shard_map(
        per_device,
        mesh=mesh,
        in_specs=placed,
        out_specs=(P("section", None, "tensor"), P("section", None, "tensor")),
        check_vma=False,
    )
```

```python
import functools

import jax
import jax.numpy as jnp
from jax import lax
from jax.experimental import pallas as pl
from jax.experimental.pallas import tpu as pltpu
from jax.sharding import PartitionSpec as P

epsilon = 1e-06
softness = 4.0
loss_scale = 4096.0
chunk_width = 1024

f32 = jnp.float32
bf16 = jnp.bfloat16


def shifted(value, axis, steps):
    count = lax.axis_size(axis)
    initial, last = (max(0, -steps), min(count, count - steps))
    return lax.ppermute(value, axis, [(source, source + steps) for source in range(initial, last)])


def rotated(value, steps):
    count = lax.axis_size("tensor")
    return lax.ppermute(value, "tensor", [(i, (i + steps) % count) for i in range(count)])


def fenced(value, after):
    return lax.optimization_barrier((value, *after))[0] if after else value


def copy_kernel(places, *refs):
    sources, targets, sems = refs[: -len(places) - 1], refs[-len(places) - 1 : -1], refs[-1]
    count, me = lax.axis_size("tensor"), lax.axis_index("tensor")
    copies = []
    for slot, (number, row, column) in enumerate(places):
        rows, columns = targets[slot].shape
        starts = []
        for size, (away, width, offset) in zip((rows, columns), (row, column)):
            start = offset if away is None else lax.rem(me + away, count) * width + offset
            starts.append(pl.ds(start if away is None else pl.multiple_of(start, 128), size))
        source = sources[number].at[starts[0], starts[1]]
        copies.append(pltpu.make_async_copy(source, targets[slot], sems.at[slot]))
    for copy in copies:
        copy.start()
    for copy in copies:
        copy.wait()


here = (None, 0, 0)


def copied(matrices, places, shapes):
    moved = sum(2 * rows * columns for rows, columns in shapes)
    anywhere = pl.BlockSpec(memory_space=pl.ANY)
    return pl.pallas_call(
        functools.partial(copy_kernel, places),
        out_shape=[jax.ShapeDtypeStruct(shape, bf16) for shape in shapes],
        in_specs=[anywhere] * len(matrices),
        out_specs=[pl.BlockSpec(memory_space=pltpu.VMEM)] * len(shapes),
        scratch_shapes=[pltpu.SemaphoreType.DMA((len(shapes),))],
        cost_estimate=pl.CostEstimate(flops=0, bytes_accessed=2 * moved, transcendentals=0),
        compiler_params=pltpu.CompilerParams(vmem_limit_bytes=32 * 1024 * 1024),
        name="copied",
    )(*matrices)


def settled(value):
    return lax.optimization_barrier(value)


def fenced_all(values, after):
    return lax.optimization_barrier((*values, *after))[: len(values)]


class Lane:
    def __init__(self, depth):
        self.depth = depth
        self.past = []

    def send(self, value, steps, after=(), depth=None):
        depth = depth or self.depth
        if len(self.past) >= depth:
            after = (self.past[-depth], *after)
        value = fenced(value, after)
        arrived = rotated(value, steps)
        self.past.append(arrived)
        return arrived


def dot(left, right):
    return jnp.dot(left, right, preferred_element_type=f32)


def dot_t(left, right):
    return lax.dot_general(left, right, (((1,), (1,)), ((), ())), preferred_element_type=f32)


def rows_at(matrix, start, size):
    return lax.dynamic_slice_in_dim(matrix, start, size, 0)


def cols_at(matrix, start, size):
    return lax.dynamic_slice_in_dim(matrix, start, size, 1)


def total(terms):
    result = terms[0]
    for term in terms[1:]:
        result = result + term
    return result


def soft_min(first, second):
    return 0.5 * (
        first + second - jnp.sqrt((first - second) * (first - second) + softness * softness)
    )


def soft_max(first, second):
    return 0.5 * (
        first + second + jnp.sqrt((first - second) * (first - second) + softness * softness)
    )


def soft_relu(difference):
    return 0.5 * (difference + jnp.sqrt(difference * difference + softness * softness))


def box_loss(logits, target):
    centre_x, centre_y, box_width, box_height = [jax.nn.sigmoid(v) * 1000.0 for v in logits]
    left, lower, right, upper = target
    left_pred = centre_x - 0.5 * box_width
    right_pred = centre_x + 0.5 * box_width
    lower_pred = centre_y - 0.5 * box_height
    upper_pred = centre_y + 0.5 * box_height
    inner_width = soft_relu(soft_min(right_pred, right) - soft_max(left_pred, left))
    inner_height = soft_relu(soft_min(upper_pred, upper) - soft_max(lower_pred, lower))
    intersection_area = inner_width * inner_height
    target_area = (right - left) * (upper - lower)
    union_area = box_width * box_height + target_area - intersection_area
    outer_width = soft_max(right_pred, right) - soft_min(left_pred, left)
    outer_height = soft_max(upper_pred, upper) - soft_min(lower_pred, lower)
    enclosing = outer_width * outer_height
    return 1.0 - intersection_area / union_area + (enclosing - union_area) / enclosing


def column(row):
    return jnp.transpose(jnp.broadcast_to(row, (128, row.shape[1])))[:, :1]


def gate_kernel(count, pairs, mine_ref, act_grad_ref, *refs):
    got_refs, refs = refs[: count - 1], refs[count - 1 :]
    left_refs, right_refs, refs = refs[:pairs], refs[pairs : 2 * pairs], refs[2 * pairs :]
    groups = mine_ref.shape[0] // act_grad_ref.shape[0]
    inverse_refs, (grad_ref, along_ref, *out_refs) = refs[:groups], refs[groups:]
    tokens = act_grad_ref.shape[0]
    pre = total([mine_ref[...]] + [ref[...].astype(f32) for ref in got_refs])
    first = pre[:tokens] * column(inverse_refs[0][...])
    gate = jax.nn.sigmoid(first)
    act_grad = total(
        [act_grad_ref[...]] + [dot_t(x[...], w[...]) for x, w in zip(left_refs, right_refs)]
    )
    grad = (act_grad * gate * (1.0 + first * (1.0 - gate))).astype(bf16)
    grad_ref[...] = grad
    along_ref[...] = lax.dot_general(
        jnp.ones((1, first.shape[1]), f32),
        grad.astype(f32) * first,
        (((1,), (1,)), ((), ())),
        precision=lax.Precision.HIGHEST,
        preferred_element_type=f32,
    )
    if groups > 1:
        second = pre[tokens:] * column(inverse_refs[1][...])
        out_refs[0][...] = (second * jax.nn.sigmoid(second)).astype(bf16)


def gated(mine, got, inverses, act_grad, left=(), right=()):
    tokens, hidden_width = act_grad.shape
    shapes = [
        jax.ShapeDtypeStruct((tokens, hidden_width), bf16),
        jax.ShapeDtypeStruct((1, tokens), f32),
    ]
    if mine.shape[0] > tokens:
        shapes.append(jax.ShapeDtypeStruct((mine.shape[0] - tokens, hidden_width), bf16))
    whole = pl.BlockSpec(memory_space=pltpu.VMEM)
    return pl.pallas_call(
        functools.partial(gate_kernel, len(got) + 1, len(left)),
        out_shape=shapes,
        in_specs=[whole] * (len(got) + 2 + 2 * len(left) + len(inverses)),
        out_specs=[whole] * len(shapes),
        compiler_params=pltpu.CompilerParams(vmem_limit_bytes=32 * 1024 * 1024),
        name="gated",
    )(mine, act_grad, *got, *left, *right, *inverses)


def head_kernel(count, full_width, *refs):
    pooled_refs, weight_refs = refs[:count], refs[count : 2 * count]
    gain_ref, bias_ref, target_ref, prompt_ref, keep_ref = refs[2 * count : 2 * count + 5]
    out_refs = refs[2 * count + 5 :]
    me = lax.axis_index("tensor")
    rows, width = pooled_refs[0].shape
    gains = []
    for k in range(count):
        start = pl.multiple_of(lax.rem(me + count - k, count) * width, width)
        gains.append(gain_ref[:, pl.ds(start, width)])
    for row in range(rows):
        weights = pool_weights(prompt_ref[row], keep_ref[row : row + 1, :])
        inverse_count = 1.0 / jnp.sum(weights, axis=1, keepdims=True)
        pooled = [ref[row : row + 1, :] * inverse_count for ref in pooled_refs]
        square = total([jnp.sum(p * p, axis=1, keepdims=True) for p in pooled])
        inverse = lax.rsqrt(square / full_width + epsilon)
        projected = inverse * total(
            [
                jnp.sum((p * g) * w[...], axis=1, keepdims=True)
                for p, g, w in zip(pooled, gains, weight_refs)
            ]
        )
        projected = [projected[j : j + 1, :] for j in range(4)]
        target = [target_ref[row, j].astype(f32) for j in range(4)]
        logits = [projected[j] + bias_ref[j] for j in range(4)]
        _, pullback = jax.vjp(lambda *values: box_loss(values, target), *logits)
        logit_grad = pullback(jnp.full((1, 1), loss_scale / rows, f32))
        row_mean = total([logit_grad[j] * projected[j] for j in range(4)]) / full_width
        for p, g, w, out in zip(pooled, gains, weight_refs, out_refs):
            scaled_grad = total([logit_grad[j] * w[j : j + 1, :] for j in range(4)])
            out[row : row + 1, :] = (
                inverse * (g * scaled_grad - p * inverse * row_mean) * inverse_count
            )


def pool_weights(prompt_length, keep_row):
    positions = lax.broadcasted_iota(jnp.int32, keep_row.shape, 1)
    starting = jnp.where(positions == prompt_length - 1, 1.0, 0.0)
    kept = jnp.where(positions >= prompt_length, 1.0, 0.0)
    return starting + kept * keep_row.astype(f32)


def head_rows(pooled, weights, head_gain, head_bias, target_box, prompt_length, keep_mask, full_width):
    count = len(pooled)
    whole = pl.BlockSpec(memory_space=pltpu.VMEM)
    scalars = pl.BlockSpec(memory_space=pltpu.SMEM)
    rows = pl.pallas_call(
        functools.partial(head_kernel, count, full_width),
        out_shape=[jax.ShapeDtypeStruct(p.shape, f32) for p in pooled],
        in_specs=[whole] * (2 * count + 1) + [scalars] * 3 + [whole],
        out_specs=[whole] * count,
        name="head",
    )(*pooled, *weights, head_gain[None, :], head_bias, target_box, prompt_length, keep_mask)
    return [row.astype(bf16) for row in rows]


def per_device(
    forward_input,
    saved_last,
    saved_first,
    first_cotangent,
    section_entry,
    last_gain,
    last_up,
    last_down,
    first_gain,
    first_up,
    first_down,
    head_gain,
    head_weight,
    head_bias,
    prompt_length,
    keep_mask,
    target_box,
):
    count = lax.axis_size("tensor")
    me = lax.axis_index("tensor")
    section_index = lax.axis_index("section")
    opening = section_index == 0
    closing = section_index == lax.axis_size("section") - 1
    entering, saved, cotangent = forward_input[0], saved_first[0], first_cotangent[0]
    last_up, last_down, first_up, first_down = last_up[0], last_down[0], first_up[0], first_down[0]
    tokens, width = entering.shape
    full_width = width * count
    hidden_width = last_up.shape[1]
    chunk = min(width, chunk_width)
    pieces = range(width // chunk)
    final = pieces[-1]
    others = range(1, count)
    after = [lax.rem(me + k, count) for k in range(count)]
    before = [lax.rem(me + count - k, count) for k in range(count)]

    def piece(values, j):
        return values[:, j * chunk : (j + 1) * chunk]

    def square_sum(values):
        values = values.astype(f32)
        return jnp.sum(values * values, axis=1)

    lane = Lane(2)
    first_gain_cols = rows_at(first_gain[0], me * width, width)
    last_gain_cols = rows_at(last_gain[0], me * width, width)

    def scaled(values, gain_cols):
        return (values.astype(f32) * gain_cols).astype(bf16)

    def gain_piece(gain_cols, j):
        return gain_cols[j * chunk : (j + 1) * chunk]

    def up_parts(up_matrix, sizes):
        starts = [sum(sizes[:cut]) for cut in range(len(sizes))]
        places = [(0, (k, width, start), here) for start in starts for k in others]
        shapes = [(size, hidden_width) for size in sizes for k in others]
        places.append((0, (0, width, 0), here))
        shapes.append((width, hidden_width))
        parts = copied([up_matrix], places, shapes)
        step = count - 1
        return [parts[i * step : (i + 1) * step] for i in range(len(sizes))], parts[-1]

    def down_parts(down_matrix):
        places = [(0, here, (k, width, 0)) for k in range(count)]
        return copied([down_matrix], places, [(hidden_width, width)] * count)

    def send_up(parts, ahead=(), depth=None):
        return [lane.send(part, k, ahead, depth) for part, k in zip(parts, others)]

    def up_rows(own, got, start, size):
        blocks = [own[start : start + size]]
        for cuts in zip(*got):
            taken, at = [], 0
            for cut in cuts:
                low, high = max(start - at, 0), min(start + size - at, cut.shape[0])
                if low < high:
                    taken.append(cut[low:high])
                at += cut.shape[0]
            blocks.append(taken[0] if len(taken) == 1 else jnp.concatenate(taken, axis=0))
        return blocks

    def exchange_cols(values, ahead=()):
        return [values] + [lane.send(values, k, ahead) for k in others]

    def sum_small(values):
        return total([values] + [rotated(values, k) for k in others])

    def collect(sent):
        return [lane.send(t, -k) for t, k in zip(sent, others)]

    def exchange_grad(pre_grad, along):
        blocks = [pre_grad] + [lane.send(pre_grad, k) for k in others]
        return blocks, sum_small(along)[0] / full_width

    def other_products(normed, got, after=()):
        sums = []
        for cuts in zip(*got):
            terms, at = [], 0
            for cut in cuts[:-1]:
                terms.append(dot(normed[:, at : at + cut.shape[0]], cut))
                at += cut.shape[0]
            early = [settled(total(terms))] if terms else []
            last = dot(fenced(normed[:, at:], [*early, *after]), cuts[-1])
            sums.append(total([*early, last]).astype(bf16))
        return sums

    def input_grad(values, given, inverse, gain_cols, blocks, along, up_blocks):
        norm_grad = total([dot_t(blocks[k], up_blocks[k]) for k in range(count)])
        unit = values.astype(f32) * inverse[:, None]
        return (
            given.astype(f32)
            + inverse[:, None] * (gain_cols * norm_grad - unit * along[:, None])
        ).astype(bf16)

    def send_out(activated, downs, j, ahead=()):
        values = [dot(activated, piece(downs[k], j)).astype(bf16) for k in others]
        depth = 3 if j < 2 else 2
        return [lane.send(value, k, ahead, depth) for value, k in zip(values, others)]

    def add_out(values, mine, terms):
        return (values.astype(f32) + total([mine] + [t.astype(f32) for t in terms])).astype(bf16)

    def act_grad_terms(blocks, downs):
        return [dot_t(blocks[k], downs[-k]) for k in range(count)]

    stored = jnp.where(closing, entering, saved_last[0])

    last_parts, last_up_own = up_parts(last_up, [width // 2] * 2)
    cotangents = exchange_cols(cotangent)
    last_got = [send_up(last_parts[0])]
    last_downs = down_parts(last_down)
    first_parts, first_up_own = up_parts(first_up, [width // 4, width // 4, width // 2])
    first_downs = down_parts(first_down)
    squares = jnp.stack([square_sum(saved), square_sum(entering), square_sum(stored)])
    head_weights = [head_weight.T]
    entering_scaled = scaled(entering, last_gain_cols)
    stored_scaled = scaled(stored, last_gain_cols)
    first_saved = scaled(saved, first_gain_cols)

    last_got.append(send_up(last_parts[1]))
    ahead = [
        *last_downs, first_up_own, *first_downs, squares, *head_weights, entering_scaled,
        stored_scaled, first_saved,
    ]
    first_got = [send_up(first_parts[0], ahead)]
    sent = other_products(entering_scaled, last_got)
    mine = dot(fenced(entering_scaled, sent), last_up_own)
    got = collect(sent)
    squares = fenced(squares, sent)
    squares = total([squares] + [rotated(squares, k) for k in others])
    inverses = lax.rsqrt(squares / full_width + epsilon)
    head_weights += [rotated(fenced(head_weights[0], sent), k) for k in others]
    act_grad = total(act_grad_terms(cotangents, first_downs))
    first_got.append(send_up(first_parts[1], sent))
    stored_sent = other_products(fenced(stored_scaled, sent), last_got)
    stored_mine = dot(fenced(stored_scaled, sent), last_up_own)
    stored_got = collect(stored_sent)
    inverse_rows = [settled(inverses[i : i + 1]) for i in range(3)]
    first_gains = [settled(gain_piece(first_gain_cols, j)) for j in pieces]
    last_up_got = [settled(jnp.concatenate(cuts, axis=0)) for cuts in zip(*last_got)]
    right = [settled(piece(last_downs[-k], final)) for k in others]
    got = fenced_all(got, [*right, *last_up_got, *stored_sent, stored_mine, act_grad, *inverse_rows, *first_gains, last_gain_cols, *head_weights[1:]])
    entering_pre = total([mine] + [t.astype(f32) for t in got]) * inverses[1][:, None]

    activated = jax.nn.silu(entering_pre).astype(bf16)
    gots = [send_out(activated, last_downs, j) for j in pieces[:-1]]
    mine = dot(activated, last_downs[0])
    gots.append(send_out(activated, last_downs, final, [mine]))
    first_got.append(send_up(first_parts[2], depth=3))
    hidden = add_out(entering, mine, [jnp.concatenate(t, axis=1) for t in zip(*gots)])
    entry = jnp.where(opening, section_entry, shifted(hidden, "section", 1))

    row_count, row_length = keep_mask.shape
    token_weights = jnp.concatenate(
        [pool_weights(prompt_length[row], keep_mask[row : row + 1]) for row in range(row_count)], 0
    )

    def pool(values):
        weights = token_weights.astype(bf16)
        if row_count == 1:
            return dot(weights, values)
        values = values.reshape(row_count, row_length, values.shape[1])
        return jnp.einsum("rt,rtd->rd", weights, values, preferred_element_type=f32)

    def on_tokens(rows):
        values = token_weights[:, :, None] * rows.astype(f32)[:, None, :]
        return values.reshape(tokens, rows.shape[1])

    pooled = pool(fenced(hidden, [entry]))

    entry_squares = sum_small(square_sum(entry)[None, :])
    entry_inverse = settled(lax.rsqrt(entry_squares / full_width + epsilon))
    pair = jnp.concatenate([first_saved, scaled(entry, first_gain_cols)], axis=0)
    sent = other_products(pair, first_got)
    mine = dot(fenced(pair, sent), first_up_own)
    got = collect(sent)
    pooled = fenced(pooled, sent)
    pooled = [pooled] + [rotated(pooled, k) for k in others]

    pre_grad, along, entry_activated = gated(mine, got, [inverse_rows[0], entry_inverse], act_grad)
    first_blocks, first_along = exchange_grad(pre_grad, along)
    early = (len(pieces) + 1) // 2

    def first_out(low, high, activated):
        columns = slice(low * chunk, high * chunk)
        values = [dot(activated, first_downs[k][:, columns]).astype(bf16) for k in others]
        return [lane.send(value, k) for value, k in zip(values, others)]

    gots = [first_out(0, early, entry_activated)]
    returned = []
    for j in pieces:
        gradient = input_grad(
            piece(saved, j),
            piece(cotangent, j),
            inverses[0],
            first_gains[j],
            fenced_all(first_blocks, returned[-1:]),
            first_along,
            up_rows(first_up_own, first_got, j * chunk, chunk),
        )
        returned.append(gradient)
    returned = [shifted(gradient, "section", -1) for gradient in returned]

    act_grads = []
    for j in pieces[:-1]:
        ahead = act_grads[j - 2 : j - 1] if j > 1 else ()
        blocks = exchange_cols(returned[j], ahead)
        terms = act_grad_terms(blocks, [piece(d, j) for d in last_downs])
        act_grads.append(total(act_grads[-1:] + terms))
        if j == 0:
            late = blocks[1:]
    if final == 0:
        late = first_blocks[1:]
    head_grads = head_rows(
        fenced_all(pooled, late),
        head_weights,
        head_gain,
        head_bias,
        target_box,
        prompt_length,
        keep_mask,
        full_width,
    )
    head_act_grad = total([dot_t(head_grads[k], last_downs[-k]) for k in range(count)])
    given = settled(
        jnp.where(
            closing, on_tokens(head_grads[0]).astype(bf16), jnp.concatenate(returned, axis=1)
        )
    )
    act_grad = settled(
        total(
            [
                jnp.where(closing, on_tokens(head_act_grad), 0.0),
                dot_t(returned[-1], piece(last_downs[0], final)),
                *act_grads[-1:],
            ]
        )
    )
    activated_late = fenced(entry_activated, late)
    if early < final:
        gots.append(first_out(early, final, activated_late))
    ahead = [given, act_grad, *right]
    left = exchange_cols(returned[-1], ahead)[1:]
    pre_grad, along = gated(stored_mine, stored_got, inverse_rows[2:], act_grad, left, right)
    last_blocks, last_along = exchange_grad(pre_grad, along)
    if early <= final:
        gots.append(first_out(max(early, final), len(pieces), activated_late))
    outs, at = [], 0
    for got in gots[:-1]:
        columns = slice(at, at + got[0].shape[1])
        mine = dot(activated_late, first_downs[0][:, columns])
        outs.append(add_out(entry[:, columns], mine, got))
        at = columns.stop
    mine = settled(dot(activated_late, first_downs[0][:, at:]))
    outs = jnp.concatenate([*outs, entry[:, at:]], axis=1)
    got = fenced_all(gots[-1], [mine, outs])
    layer_output = lax.dynamic_update_slice_in_dim(outs, add_out(entry[:, at:], mine, got), at, 1)

    own = settled(dot_t(last_blocks[0], last_up_own))
    norm_grad = total(
        [own] + [dot_t(block, got) for block, got in zip(last_blocks[1:], last_up_got)]
    )
    unit = stored.astype(f32) * inverses[2][:, None]
    input_gradient = (
        given.astype(f32)
        + inverses[2][:, None] * (last_gain_cols * norm_grad - unit * last_along[:, None])
    ).astype(bf16)
    return (layer_output[None], input_gradient[None])


def solution(mesh):
    placed = (
        P("section", None, "tensor"),
        P("section", None, "tensor"),
        P("section", None, "tensor"),
        P("section", None, "tensor"),
        P(None, "tensor"),
        P("section", None),
        P("section", None, "tensor"),
        P("section", "tensor", None),
        P("section", None),
        P("section", None, "tensor"),
        P("section", "tensor", None),
        P(),
        P("tensor", None),
        P(),
        P(),
        P(),
        P(),
    )
    return jax.shard_map(
        per_device,
        mesh=mesh,
        in_specs=placed,
        out_specs=(P("section", None, "tensor"), P("section", None, "tensor")),
        check_vma=False,
    )
```
